128 devices in a mesh: row: 8 (over z, core), col: 16 (over x, y).
Axes of the slice: x: 4, y: 4, z: 4, core: 2. Of those that a mesh axis runs over, the one named last changes fastest.
Arguments:
- features: float32 [24576, 128], P(('row', 'col')), may hold values from -6 to 6
- squared_scales: float32 [128], replicated, may hold values from 64 to 256
- noise_var: float32 [24576], P(('row', 'col')), may hold values from 0.05 to 0.5
- signal: float32 [1], replicated, may hold values from 0.5 to 2
Outputs:
- updated: float32 [24576, 24576], P('row', 'col')
- panel_out: float32 [24576, 256], P('row')
The draws below stay inside these ranges and needn't reach their ends.
All inputs are finite; a program needn't handle non-finite values.
Results may differ from the reference program's by a relative error of at most 0.0003.
Values sent between devices are 32-bit elements; how exact they have to be, the bound alone decides.
A program may use at most 128 MiB of HBM per device.

```python
import math
import jax
import jax.numpy as jnp
from jax import lax

F = 128
B = 256
ROWS_DEV = 3072
N = 24576
N_ROW = 8


def levels(own_key, shape, cuts, low, high):
    factor_of, own = 1.0, jax.random.fold_in(own_key, 6)
    for axis_at, shards_of in cuts:
        heights = jnp.exp(jax.random.uniform(jax.random.fold_in(own, axis_at), (shards_of,), jnp.float32, low / len(cuts), high / len(cuts)))
        factor_of = factor_of * jnp.repeat(heights, shape[axis_at] // shards_of).reshape([-1 if axis == axis_at else 1 for axis in range(len(shape))])
    return factor_of


def scatter_about(stream_key, shape, scale, most, cuts=(), kind=jnp.bfloat16):
    entries = jax.random.normal(stream_key, shape, jnp.float32) * scale
    if len(cuts) > 0:
        entries = levels(stream_key, shape, cuts, -0.22, 0.18) * entries
    return jnp.clip(entries, min=-most, max=most).astype(kind)


def setup_inputs(seed: int = 0) -> dict:
    seeds = jax.random.split(jax.random.key(seed), 5)
    features = scatter_about(seeds[0], (N, F), 1.0, 6.0, ((0, 128),), jnp.float32)
    squared_scales = jnp.clip(jnp.exp(jax.random.uniform(seeds[1], (F,), jnp.float32, math.log(64.0), math.log(256.0))), 64.0, 256.0)
    noise_var = jnp.clip(jnp.exp(math.log(0.5) - 2.3025851 * jax.random.uniform(seeds[2], (N,), jnp.float32) ** levels(seeds[2], (N,), ((0, 128),), -0.2, 0.2)), 0.05, 0.5)
    signal = jnp.clip(jnp.exp(jax.random.uniform(seeds[3], (1,), jnp.float32, math.log(0.5), math.log(2.0))), 0.5, 2.0)
    return {"features": features, "squared_scales": squared_scales, "noise_var": noise_var, "signal": signal}


def kernel_block(left, right, left_sq, right_sq, signal):
    products = jnp.dot(left.astype(jnp.float32), right.T.astype(jnp.float32), precision=lax.Precision.HIGHEST, preferred_element_type=jnp.float32)
    distance = jnp.maximum(left_sq[:, None] + right_sq[None, :] - 2.0 * products, 0.0)
    reach = jnp.sqrt(5.0 * distance)
    return signal[0] * (1.0 + reach + reach * reach / 3.0) * jnp.exp(-reach)

def reference(features, squared_scales, noise_var, signal):
    scaled = features / jnp.sqrt(squared_scales)[None, :]
    sq_norms = lax.optimization_barrier(jnp.sum(scaled * scaled, axis=1))
    count_all = scaled.shape[0]
    pivot_rows = scaled[:B]
    pivot_sq = sq_norms[:B]
    pivot_index = jnp.arange(B, dtype=jnp.int32)
    all_index = jnp.arange(count_all, dtype=jnp.int32)
    pivot_block = kernel_block(pivot_rows, pivot_rows, pivot_sq, pivot_sq, signal)
    pivot_block = pivot_block + jnp.where(pivot_index[:, None] == pivot_index[None, :], noise_var[:B][:, None], 0.0)
    factor = jnp.linalg.cholesky(pivot_block)
    column = kernel_block(scaled, pivot_rows, sq_norms, pivot_sq, signal)
    column = column + jnp.where(all_index[:, None] == pivot_index[None, :], noise_var[:, None], 0.0)
    panel_out = lax.linalg.triangular_solve(factor, column, left_side=False, lower=True, transpose_a=True)

    def one_block(offset):
        block_rows = lax.dynamic_slice_in_dim(scaled, offset, ROWS_DEV, 0)
        block_sq = lax.dynamic_slice_in_dim(sq_norms, offset, ROWS_DEV, 0)
        block_noise = lax.dynamic_slice_in_dim(noise_var, offset, ROWS_DEV, 0)
        block_panel = lax.dynamic_slice_in_dim(panel_out, offset, ROWS_DEV, 0)
        row_global = offset + jnp.arange(ROWS_DEV, dtype=jnp.int32)
        tile_block = kernel_block(block_rows, scaled, block_sq, sq_norms, signal)
        tile_block = tile_block + jnp.where(row_global[:, None] == all_index[None, :], block_noise[:, None], 0.0)
        return tile_block - jnp.dot(block_panel.astype(jnp.float32), panel_out.T.astype(jnp.float32), precision=lax.Precision.HIGHEST, preferred_element_type=jnp.float32)
    offsets = jnp.arange(N_ROW, dtype=jnp.int32) * ROWS_DEV
    updated = lax.map(one_block, offsets).reshape(count_all, count_all)
    return (updated, panel_out)
```

```python
import functools
import math

import jax
import jax.numpy as jnp
from jax import lax
from jax.experimental import pallas as pl
from jax.experimental.pallas import tpu as pltpu
from jax.sharding import PartitionSpec as P

MESH = pl.DeviceIdType.MESH
F = 128
B = 256
OWN = 192
BLOCK = 200
PIECE = 24
N_ROW = 8
N_COL = 16
NB = 32
TILE = 384
CHUNK = 512
FOLD = math.sqrt(5.0) / math.log(2.0)
LN2 = math.log(2.0)
BF16 = jnp.bfloat16
F32 = jnp.float32


def split2(a):
    high = a.astype(BF16)
    return high, (a - high.astype(F32)).astype(BF16)


def split3(a):
    high = a.astype(BF16)
    rest = a - high.astype(F32)
    mid = rest.astype(BF16)
    return high, mid, (rest - mid.astype(F32)).astype(BF16)


def mm(a, b):
    return jnp.dot(a, b, preferred_element_type=F32)


def left_operand(scaled):
    n = scaled.shape[0]
    sq = jnp.sum(scaled * scaled, axis=1, keepdims=True)
    high, low = split2(scaled * -2.0)
    one, two, three = split3(jnp.broadcast_to(sq, (n, F)))
    lane = lax.broadcasted_iota(jnp.int32, (n, F), 1)
    extra = jnp.where(
        lane == 0,
        one.astype(F32),
        jnp.where(
            lane == 1,
            two.astype(F32),
            jnp.where(lane == 2, three.astype(F32), jnp.where(lane < 6, 1.0, 0.0)),
        ),
    ).astype(BF16)
    return jnp.concatenate([high, low, high, extra], axis=1)


def right_operand(scaled_t):
    n = scaled_t.shape[1]
    sq = jnp.sum(scaled_t * scaled_t, axis=0, keepdims=True)
    high, low = split2(scaled_t)
    one, two, three = split3(jnp.broadcast_to(sq, (F, n)))
    sub = lax.broadcasted_iota(jnp.int32, (F, n), 0)
    extra = jnp.where(
        sub < 3,
        1.0,
        jnp.where(
            sub == 3,
            one.astype(F32),
            jnp.where(
                sub == 4,
                two.astype(F32),
                jnp.where(sub == 5, three.astype(F32), 0.0),
            ),
        ),
    ).astype(BF16)
    return jnp.concatenate([high, high, low, extra], axis=0)


def matern(u2, signal):
    a = jnp.maximum(u2, 1e-30)
    u = a * lax.rsqrt(a)
    poly = signal + u * (signal * LN2 + u * (signal * (LN2 * LN2 / 3.0)))
    return poly * jnp.exp2(-u)


def pivot_noise(tile0, tile1):
    first = tile0[0:1, :]
    second = jnp.concatenate([tile0[1:2, 0:64], tile1[0:1, 0:64]], axis=1)
    return jnp.concatenate([first, second], axis=1)


def gather_kernel(
    feat_ref, noise_ref, scale_ref, signal_ref,
    rows_ref, cols_ref, piv_ref, w_ref,
    stage, zbuf, aug,
    s1_send, s1_recv, s2_send, s2_recv, s3_send, s3_recv,
    row_send, row_recv, z_send, z_recv, xy_send, cols_recv,
):
    r = lax.axis_index("row")
    c = lax.axis_index("col")
    z = r // 2
    core = r % 2
    x = c // 4
    y = c % 4
    sib = z * 2 + (1 - core)

    barrier = pltpu.get_barrier_semaphore()

    def signal_to(rr, cc):
        pl.semaphore_signal(barrier, inc=1, device_id=(rr, cc), device_id_type=MESH)

    def greet_row(k, carry):
        signal_to(r, (c + k) % N_COL)
        return carry

    def greet_sib(k, carry):
        signal_to(sib, (c + k) % N_COL)
        return carry

    def greet_z(k, carry):
        signal_to(((z + k) % 4) * 2, c)
        signal_to(((z + k) % 4) * 2 + 1, c)
        return carry

    lax.fori_loop(1, N_COL, greet_row, 0)
    lax.fori_loop(0, N_COL, greet_sib, 0)
    lax.fori_loop(1, 4, greet_z, 0)

    rows_ref[c, 0:OWN, :] = feat_ref[...]
    rows_ref[c, OWN:BLOCK, :] = jnp.zeros((BLOCK - OWN, F), F32)
    rows_ref[c, OWN:OWN + 1, :] = noise_ref[0:1, 0:F]
    rows_ref[c, OWN + 1:OWN + 2, 0:64] = noise_ref[0:1, F:OWN]
    tile = rows_ref[c, OWN:BLOCK, :]
    for q in range(12):
        stage[q, 0:16, :] = feat_ref[16 * q:16 * q + 16, :]
        stage[q, 16:PIECE, :] = tile

    pl.semaphore_wait(barrier, 15 + 16 + 6)

    def remote(src, dst, send, recv, rr, cc):
        return pltpu.make_async_remote_copy(
            src_ref=src, dst_ref=dst, send_sem=send, recv_sem=recv,
            device_id=(rr, cc), device_id_type=MESH,
        )

    def s1_copy(q, target):
        return remote(stage.at[q], piv_ref.at[target], s1_send.at[q], s1_recv, 0, target)

    @pl.when((r == 0) & (c == 0))
    def _():
        def go(q, carry):
            s1_copy(q, q).start()
            return carry
        lax.fori_loop(1, 12, go, 0)
        piv_ref[0] = stage[0]

    @pl.when((r == 0) & (c == 1))
    def _():
        def go(q, carry):
            s1_copy(q, 12 + q).start()
            return carry
        lax.fori_loop(0, 4, go, 0)

    @pl.when((r == 0) & (c != 0))
    def _():
        s1_copy(0, c).wait_recv()

    def s2_copy(k):
        return remote(piv_ref.at[c], piv_ref.at[c], s2_send.at[k], s2_recv, k, c)

    @pl.when(r == 0)
    def _():
        def go(k, carry):
            s2_copy(k).start()
            return carry
        lax.fori_loop(1, N_ROW, go, 0)

    def z_copy(k):
        return remote(
            rows_ref.at[c], zbuf.at[z], z_send.at[k], z_recv.at[z], ((z + k) % 4) * 2 + core, c
        )

    @pl.when(r != 0)
    def _():
        s2_copy(0).wait_recv()

    def peer(k):
        return ((x + k // 4) % 4) * 4 + (y + k % 4) % 4

    def s3_copy(k, slot):
        return remote(piv_ref.at[slot], piv_ref.at[slot], s3_send.at[k], s3_recv.at[slot], r, peer(k))

    def s3_go(k, carry):
        s3_copy(k, c).start()
        return carry

    lax.fori_loop(1, N_COL, s3_go, 0)

    def z_go(k, carry):
        z_copy(k).start()
        return carry

    lax.fori_loop(1, 4, z_go, 0)

    def row_copy(k, slot):
        return remote(rows_ref.at[slot], rows_ref.at[slot], row_send.at[k], row_recv.at[slot], r, peer(k))

    def row_go(k, carry):
        row_copy(k, c).start()
        return carry

    lax.fori_loop(1, N_COL, row_go, 0)

    def s3_wait(k, carry):
        s3_copy(k, peer(k)).wait_recv()
        return carry

    lax.fori_loop(1, N_COL, s3_wait, 0)

    signal = signal_ref[0, 0]
    scale = lax.rsqrt(scale_ref[...]) * FOLD
    pivots = jnp.concatenate([piv_ref[p, 0:16, :] for p in range(16)], axis=0) * scale
    u2 = mm(left_operand(pivots), right_operand(pivots.T))
    row_id = lax.broadcasted_iota(jnp.int32, (B, B), 0)
    col_id = lax.broadcasted_iota(jnp.int32, (B, B), 1)
    noise = pivot_noise(piv_ref[0, 16:PIECE, :], piv_ref[12, 16:PIECE, :])
    aug[:, 0:B] = matern(u2, signal) + jnp.where(row_id == col_id, noise, 0.0)
    aug[:, B:2 * B] = jnp.where(row_id == col_id, 1.0, 0.0)

    def z_wait(k, carry):
        z_from = (z + k) % 4
        remote(
            rows_ref.at[c], zbuf.at[z_from], z_send.at[0], z_recv.at[z_from], r, c
        ).wait_recv()
        return carry

    lax.fori_loop(1, 4, z_wait, 0)

    index = c % 8

    def xy_copy(k, m):
        source = (z + k) % 4
        target = 2 * (2 * source + core) + c // 8
        return source, target, 2 * z + m

    def xy_each(k, m, act):
        source, target, to_row = xy_copy(k, m)
        mine = (target == c) & (to_row == r)
        slot = k * 2 + m
        for own in (True, False):
            src = rows_ref.at[c] if own else zbuf.at[source]
            is_own = (k == 0) if own else (k != 0)

            @pl.when(is_own & mine)
            def _():
                act(pltpu.make_async_copy(src, cols_ref.at[index], cols_recv.at[index]), True)

            @pl.when(is_own & jnp.logical_not(mine))
            def _():
                act(
                    remote(src, cols_ref.at[index], xy_send.at[slot], cols_recv.at[index], to_row, target),
                    False,
                )

    def xy_go(k, carry):
        xy_each(k, 0, lambda copy, local: copy.start())
        xy_each(k, 1, lambda copy, local: copy.start())
        return carry

    lax.fori_loop(0, 4, xy_go, 0)

    sub8 = lax.broadcasted_iota(jnp.int32, (8, F), 0)

    def block_step(step, carry):
        base = pl.multiple_of(step * NB, NB)
        half = step // 4
        shift = lax.rem(F - NB * lax.rem(step, 4), F)
        group = aug[pl.ds(base, NB), pl.ds(pl.multiple_of(half * F, F), F)]
        group = pltpu.roll(group, shift, 1)
        rep = [
            [jnp.broadcast_to(group[8 * g:8 * g + 8, i:i + 1], (8, F)) if g >= i // 8 else None for g in range(4)]
            for i in range(NB)
        ]
        panel = [aug[pl.ds(base + 8 * g, 8), :] for g in range(4)]
        root = []
        for j in range(NB):
            gj, sj = divmod(j, 8)
            pivot = jnp.broadcast_to(rep[j][gj][sj:sj + 1, :], (8, F))
            inverse = 1.0 / pivot
            root.append(lax.rsqrt(pivot))
            mult = [rep[j][g] * inverse if g >= gj else None for g in range(4)]
            for i in range(j + 1, NB):
                gi, si = divmod(i, 8)
                entry = jnp.broadcast_to(rep[j][gi][si:si + 1, :], (8, F))
                for g in range(gi, 4):
                    rep[i][g] = rep[i][g] - entry * mult[g]
            line = jnp.broadcast_to(panel[gj][sj:sj + 1, :], (8, 2 * B))
            for g in range(gj, 4):
                factor = mult[g]
                if g == gj:
                    factor = jnp.where(sub8 > sj, factor, 0.0)
                panel[g] = panel[g] - jnp.concatenate([factor] * 4, axis=1) * line
        out = []
        for g in range(4):
            scale_rows = root[8 * g]
            for s in range(1, 8):
                scale_rows = jnp.where(sub8 == s, root[8 * g + s], scale_rows)
            out.append(panel[g] * jnp.concatenate([scale_rows] * 4, axis=1))
        block = jnp.concatenate(out, axis=0)
        w_ref[pl.ds(base, NB), :] = block[:, B:2 * B]
        aug[...] -= jnp.dot(
            block[:, 0:B].T, block, precision=lax.Precision.HIGHEST, preferred_element_type=F32
        )
        return carry

    lax.fori_loop(0, B // NB, block_step, 0)

    def row_wait(k, carry):
        row_copy(k, peer(k)).wait_recv()
        row_copy(k, c).wait_send()
        s3_copy(k, c).wait_send()
        return carry

    lax.fori_loop(1, N_COL, row_wait, 0)

    def z_wait_send(k, carry):
        z_copy(k).wait_send()
        return carry

    lax.fori_loop(1, 4, z_wait_send, 0)

    def cols_wait(i, carry):
        pltpu.make_async_copy(rows_ref.at[c], cols_ref.at[i], cols_recv.at[i]).wait()
        return carry

    lax.fori_loop(0, 8, cols_wait, 0)

    def xy_wait_send(k, carry):
        def act(copy, local):
            if not local:
                copy.wait_send()
        xy_each(k, 0, act)
        xy_each(k, 1, act)
        return carry

    lax.fori_loop(0, 4, xy_wait_send, 0)

    @pl.when((r == 0) & (c == 0))
    def _():
        def go(q, carry):
            s1_copy(q, q).wait_send()
            return carry
        lax.fori_loop(1, 12, go, 0)

    @pl.when((r == 0) & (c == 1))
    def _():
        def go(q, carry):
            s1_copy(q, 12 + q).wait_send()
            return carry
        lax.fori_loop(0, 4, go, 0)

    @pl.when(r == 0)
    def _():
        def go(k, carry):
            s2_copy(k).wait_send()
            return carry
        lax.fori_loop(1, N_ROW, go, 0)


def gather(features, noise, scales, signal):
    vmem = pl.BlockSpec(memory_space=pltpu.VMEM)
    smem = pl.BlockSpec(memory_space=pltpu.SMEM)
    dma = pltpu.SemaphoreType.DMA
    return pl.pallas_call(
        gather_kernel,
        out_shape=(
            jax.ShapeDtypeStruct((N_COL, BLOCK, F), F32),
            jax.ShapeDtypeStruct((8, BLOCK, F), F32),
            jax.ShapeDtypeStruct((16, PIECE, F), F32),
            jax.ShapeDtypeStruct((B, B), F32),
        ),
        in_specs=[vmem, vmem, vmem, smem],
        out_specs=(vmem,) * 4,
        scratch_shapes=[
            pltpu.VMEM((12, PIECE, F), F32),
            pltpu.VMEM((4, BLOCK, F), F32),
            pltpu.VMEM((B, 2 * B), F32),
            dma((12,)), dma, dma((8,)), dma, dma((16,)), dma((16,)),
            dma((16,)), dma((16,)), dma((4,)), dma((4,)), dma((8,)), dma((8,)),
        ],
        compiler_params=pltpu.CompilerParams(
            collective_id=0, has_side_effects=True, vmem_limit_bytes=40 * 1024 * 1024
        ),
        cost_estimate=pl.CostEstimate(flops=10**8, bytes_accessed=10**7, transcendentals=0),
    )(features, noise, scales, signal)


def update_kernel(
    rows_ref, cols_ref, piv_ref, w_ref, scale_ref, signal_ref,
    out_ref, panel_ref,
    right_d, right_p, right_piv, right_w,
):
    t = pl.program_id(0)
    r = lax.axis_index("row")
    c = lax.axis_index("col")
    signal = signal_ref[0, 0]
    scale = lax.rsqrt(scale_ref[...]) * FOLD

    def noise_line():
        return pivot_noise(piv_ref[0, 16:PIECE, :], piv_ref[12, 16:PIECE, :])

    @pl.when(t == 0)
    def _():
        pivots = jnp.concatenate([piv_ref[p, 0:16, :] for p in range(16)], axis=0) * scale
        right_piv[...] = right_operand(pivots.T)
        left = left_operand(pivots)
        for i in range(4):
            cols = jnp.concatenate([cols_ref[2 * i, 0:OWN, :], cols_ref[2 * i + 1, 0:OWN, :]], axis=0) * scale
            right_d[:, TILE * i:TILE * (i + 1)] = right_operand(cols.T)
        w = w_ref[...]
        w_high, w_low = split2(w)
        wt_high, wt_low = split2(w.T)
        right_w[...] = jnp.concatenate([wt_high, wt_high, wt_low], axis=0)
        w3 = jnp.concatenate([w_high, w_low, w_high], axis=1)
        for i in range(3):
            span = slice(CHUNK * i, CHUNK * (i + 1))
            k_pc = matern(mm(left, right_d[:, span]), signal)
            if i == 0:
                row_id = lax.broadcasted_iota(jnp.int32, (B, CHUNK), 0)
                col_id = lax.broadcasted_iota(jnp.int32, (B, CHUNK), 1)
                line = jnp.concatenate([noise_line()] * 2, axis=1)
                k_pc = k_pc + jnp.where((row_id == col_id) & (c == 0), line, 0.0)
            k_high, k_low = split2(k_pc)
            p_high, p_low = split2(mm(w3, jnp.concatenate([k_high, k_high, k_low], axis=0)))
            right_p[:, span] = jnp.concatenate([p_high, p_high, p_low], axis=0)

    rows = jnp.concatenate([rows_ref[0, 0:OWN, :], rows_ref[1, 0:OWN, :]], axis=0) * scale
    left_d = left_operand(rows)
    k_rp = matern(mm(left_d, right_piv[...]), signal)
    row_id = lax.broadcasted_iota(jnp.int32, (TILE, B), 0)
    col_id = lax.broadcasted_iota(jnp.int32, (TILE, B), 1)
    k_rp = k_rp + jnp.where((row_id == col_id) & (t == 0) & (r == 0), noise_line(), 0.0)
    k_high, k_low = split2(k_rp)
    panel = mm(jnp.concatenate([k_high, k_low, k_high], axis=1), right_w[...])
    panel_ref[...] = panel
    p_high, p_low = split2(-panel)
    left_p = jnp.concatenate([p_high, p_low, p_high], axis=1)
    for i in range(3):
        span = slice(CHUNK * i, CHUNK * (i + 1))
        k = matern(mm(left_d, right_d[:, span]), signal)
        out_ref[:, span] = k + mm(left_p, right_p[:, span])

    first = t - (c % 2) * 4

    @pl.when((r == c // 2) & (first >= 0) & (first < 4))
    def _():
        at = pl.multiple_of(first * TILE, TILE)
        lines = []
        for k in range(2):
            turned = rows_ref[k, OWN:BLOCK, :].T
            lines += [turned[:, 0:1], turned[0:64, 1:2]]
        column = jnp.concatenate(lines, axis=0)
        row_id = lax.broadcasted_iota(jnp.int32, (TILE, TILE), 0)
        col_id = lax.broadcasted_iota(jnp.int32, (TILE, TILE), 1)
        out_ref[:, pl.ds(at, TILE)] += jnp.where(row_id == col_id, column, 0.0)


def update(rows, cols, piv, w, scales, signal):
    steps = N_COL // 2
    whole = lambda shape: pl.BlockSpec(shape, lambda t: (0,) * len(shape))
    return pl.pallas_call(
        update_kernel,
        grid=(steps,),
        out_shape=(
            jax.ShapeDtypeStruct((N_COL * OWN, 8 * OWN), F32),
            jax.ShapeDtypeStruct((N_COL * OWN, B), F32),
        ),
        in_specs=[
            pl.BlockSpec((2, BLOCK, F), lambda t: (t, 0, 0)),
            whole((8, BLOCK, F)),
            whole((16, PIECE, F)),
            whole((B, B)),
            whole((1, F)),
            pl.BlockSpec(memory_space=pltpu.SMEM),
        ],
        out_specs=(
            pl.BlockSpec((TILE, 8 * OWN), lambda t: (t, 0)),
            pl.BlockSpec((TILE, B), lambda t: (t, 0)),
        ),
        scratch_shapes=[
            pltpu.VMEM((4 * F, 8 * OWN), BF16),
            pltpu.VMEM((3 * B, 8 * OWN), BF16),
            pltpu.VMEM((4 * F, B), BF16),
            pltpu.VMEM((3 * B, B), BF16),
        ],
        compiler_params=pltpu.CompilerParams(vmem_limit_bytes=56 * 1024 * 1024),
        cost_estimate=pl.CostEstimate(flops=12 * 10**9, bytes_accessed=25 * 10**6, transcendentals=10**7),
    )(rows, cols, piv, w, scales, signal)


def local(features, squared_scales, noise_var, signal):
    scales = squared_scales.reshape(1, F)
    signal = signal.reshape(1, 1)
    rows, cols, piv, w = gather(features, noise_var.reshape(1, OWN), scales, signal)
    return update(rows, cols, piv, w, scales, signal)


def solution(mesh):
    return jax.shard_map(
        local,
        mesh=mesh,
        in_specs=(P(("row", "col"), None), P(), P(("row", "col")), P()),
        out_specs=(P("row", "col"), P("row", None)),
        check_vma=False,
    )
```

```python
import functools
import math

import jax
import jax.numpy as jnp
from jax import lax
from jax.experimental import pallas as pl
from jax.experimental.pallas import tpu as pltpu
from jax.sharding import PartitionSpec as P

MESH = pl.DeviceIdType.MESH
F = 128
B = 256
OWN = 192
BLOCK = 200
PIECE = 24
N_ROW = 8
N_COL = 16
NB = 32
TILE = 384
STEPS = 8
COLS = 1536
HALF = 96
FOLD = math.sqrt(5.0) / math.log(2.0)
LN2 = math.log(2.0)
BF16 = jnp.bfloat16
F32 = jnp.float32


def split2(a):
    high = a.astype(BF16)
    return high, (a - high.astype(F32)).astype(BF16)


def split3(a):
    high = a.astype(BF16)
    rest = a - high.astype(F32)
    mid = rest.astype(BF16)
    return high, mid, (rest - mid.astype(F32)).astype(BF16)


def mm(a, b):
    return jnp.dot(a, b, preferred_element_type=F32)


def left_operand(scaled):
    n = scaled.shape[0]
    sq = jnp.sum(scaled * scaled, axis=1, keepdims=True)
    high, low = split2(scaled * -2.0)
    one, two, three = split3(jnp.broadcast_to(sq, (n, F)))
    lane = lax.broadcasted_iota(jnp.int32, (n, F), 1)
    extra = jnp.where(
        lane == 0,
        one.astype(F32),
        jnp.where(
            lane == 1,
            two.astype(F32),
            jnp.where(lane == 2, three.astype(F32), jnp.where(lane < 6, 1.0, 0.0)),
        ),
    ).astype(BF16)
    return jnp.concatenate([high, low, high, extra], axis=1)


def right_operand(scaled_t):
    n = scaled_t.shape[1]
    sq = jnp.sum(scaled_t * scaled_t, axis=0, keepdims=True)
    high, low = split2(scaled_t)
    one, two, three = split3(jnp.broadcast_to(sq, (F, n)))
    sub = lax.broadcasted_iota(jnp.int32, (F, n), 0)
    extra = jnp.where(
        sub < 3,
        1.0,
        jnp.where(
            sub == 3,
            one.astype(F32),
            jnp.where(
                sub == 4,
                two.astype(F32),
                jnp.where(sub == 5, three.astype(F32), 0.0),
            ),
        ),
    ).astype(BF16)
    return jnp.concatenate([high, high, low, extra], axis=0)


def matern(u2, signal):
    a = jnp.maximum(u2, 1e-30)
    u = a * lax.rsqrt(a)
    poly = signal + u * (signal * LN2 + u * (signal * (LN2 * LN2 / 3.0)))
    return poly * jnp.exp2(-u)


def pivot_noise(tile0, tile1):
    first = tile0[0:1, :]
    second = jnp.concatenate([tile0[1:2, 0:64], tile1[0:1, 0:64]], axis=1)
    return jnp.concatenate([first, second], axis=1)


def remote(src, dst, send, recv, rr, cc):
    return pltpu.make_async_remote_copy(
        src_ref=src, dst_ref=dst, send_sem=send, recv_sem=recv,
        device_id=(rr, cc), device_id_type=MESH,
    )


def loop(low, high, body):
    def step(k, carry):
        body(k)
        return carry

    lax.fori_loop(low, high, step, 0)


def eliminate(aug, w_ref, between):
    sub8 = lax.broadcasted_iota(jnp.int32, (8, F), 0)

    def block_step(step):
        between(step)
        base = pl.multiple_of(step * NB, NB)
        half = step // 4
        shift = lax.rem(F - NB * lax.rem(step, 4), F)
        group = aug[pl.ds(base, NB), pl.ds(pl.multiple_of(half * F, F), F)]
        group = pltpu.roll(group, shift, 1)
        rep = [
            [
                jnp.broadcast_to(group[8 * g:8 * g + 8, i:i + 1], (8, F)) if g >= i // 8 else None
                for g in range(4)
            ]
            for i in range(NB)
        ]
        panel = [aug[pl.ds(base + 8 * g, 8), :] for g in range(4)]
        root = []
        for j in range(NB):
            gj, sj = divmod(j, 8)
            pivot = jnp.broadcast_to(rep[j][gj][sj:sj + 1, :], (8, F))
            inverse = 1.0 / pivot
            root.append(lax.rsqrt(pivot))
            mult = [rep[j][g] * inverse if g >= gj else None for g in range(4)]
            for i in range(j + 1, NB):
                gi, si = divmod(i, 8)
                entry = jnp.broadcast_to(rep[j][gi][si:si + 1, :], (8, F))
                for g in range(gi, 4):
                    rep[i][g] = rep[i][g] - entry * mult[g]
            line = jnp.broadcast_to(panel[gj][sj:sj + 1, :], (8, 2 * B))
            for g in range(gj, 4):
                factor = mult[g]
                if g == gj:
                    factor = jnp.where(sub8 > sj, factor, 0.0)
                panel[g] = panel[g] - jnp.concatenate([factor] * 4, axis=1) * line
        out = []
        for g in range(4):
            scale_rows = root[8 * g]
            for s in range(1, 8):
                scale_rows = jnp.where(sub8 == s, root[8 * g + s], scale_rows)
            out.append(panel[g] * jnp.concatenate([scale_rows] * 4, axis=1))
        block = jnp.concatenate(out, axis=0)
        w_ref[pl.ds(base, NB), :] = block[:, B:2 * B]
        aug[...] -= jnp.dot(
            block[:, 0:B].T, block, precision=lax.Precision.HIGHEST, preferred_element_type=F32
        )

    loop(0, B // NB, block_step)


def gather_kernel(
    feat_hbm, noise_hbm, scale_hbm, signal_ref,
    rows_ref, cols_ref, piv_ref, w_ref,
    stage, zbuf, aug, noise_ref, scale_ref,
    in_sem, s1_send, s1_recv, s2_send, s2_recv, s3_send, s3_recv,
    p1_send, h0_send, h1_send, h0_recv, h1_recv,
    z_send, z_recv, xy_send, cols_recv, sib_send,
):
    r = lax.axis_index("row")
    c = lax.axis_index("col")
    z = r // 2
    core = r % 2
    x = c // 4
    y = c % 4
    sib = z * 2 + (1 - core)
    index = c % 8

    in_copies = (
        pltpu.make_async_copy(feat_hbm, zbuf.at[z, pl.ds(0, OWN), :], in_sem.at[0]),
        pltpu.make_async_copy(feat_hbm, rows_ref.at[c], in_sem.at[1]),
        pltpu.make_async_copy(noise_hbm, noise_ref, in_sem.at[2]),
        pltpu.make_async_copy(scale_hbm, scale_ref, in_sem.at[3]),
    )
    for copy in in_copies:
        copy.start()

    barrier = pltpu.get_barrier_semaphore()

    def signal_to(rr, cc):
        pl.semaphore_signal(barrier, inc=1, device_id=(rr, cc), device_id_type=MESH)

    def greet_z(k):
        signal_to(((z + k) % 4) * 2, c)
        signal_to(((z + k) % 4) * 2 + 1, c)

    loop(1, N_COL, lambda k: signal_to(r, (c + k) % N_COL))
    loop(1, 4, greet_z)
    loop(0, N_COL, lambda k: signal_to(sib, (c + k) % N_COL))

    for copy in in_copies:
        copy.wait()
    zbuf[z, OWN:BLOCK, :] = jnp.zeros((BLOCK - OWN, F), F32)
    zbuf[z, OWN:OWN + 1, :] = noise_ref[0:1, 0:F]
    zbuf[z, OWN + 1:OWN + 2, 0:64] = noise_ref[0:1, F:OWN]

    @pl.when((r == 0) & (c < 2))
    def _():
        tile = zbuf[z, OWN:BLOCK, :]
        for q in range(12):
            stage[q, 0:16, :] = zbuf[z, 16 * q:16 * q + 16, :]
            stage[q, 16:PIECE, :] = tile

    pl.semaphore_wait(barrier, 15 + 16 + 6)

    def s1_copy(q, target):
        return remote(stage.at[q], piv_ref.at[target], s1_send.at[q], s1_recv, 0, target)

    @pl.when((r == 0) & (c == 0))
    def _():
        loop(1, 12, lambda q: s1_copy(q, q).start())
        piv_ref[0] = stage[0]

    @pl.when((r == 0) & (c == 1))
    def _():
        loop(0, 4, lambda q: s1_copy(q, 12 + q).start())

    def s2_copy(k):
        return remote(piv_ref.at[c], piv_ref.at[c], s2_send.at[k], s2_recv, k, c)

    @pl.when((r == 0) & (c != 0))
    def _():
        s1_copy(0, c).wait_recv()

    @pl.when(r == 0)
    def _():
        loop(1, N_ROW, lambda k: s2_copy(k).start())

    def x_at(k):
        return ((x + k) % 4) * 4 + y

    def y_at(k):
        return x * 4 + (y + k) % 4

    def top(slot):
        return rows_ref.at[slot, pl.ds(0, HALF), :]

    def low(slot):
        return rows_ref.at[slot, pl.ds(HALF, HALF), :]

    def top_along_x(k):
        return remote(top(c), top(c), p1_send.at[k], h0_recv.at[c], r, x_at(k))

    def low_along_y(k):
        return remote(low(c), low(c), p1_send.at[4 + k], h1_recv.at[c], r, y_at(k))

    def top_along_y(i, k):
        slot = x_at(i)
        return remote(top(slot), top(slot), h0_send.at[4 * i + k], h0_recv.at[slot], r, y_at(k))

    def low_along_x(i, k):
        slot = y_at(i)
        return remote(low(slot), low(slot), h1_send.at[4 * i + k], h1_recv.at[slot], r, x_at(k))

    def first_go(k):
        top_along_x(k).start()
        low_along_y(k).start()

    loop(1, 4, first_go)

    @pl.when(r != 0)
    def _():
        s2_copy(0).wait_recv()

    def peer(k):
        return ((x + k // 4) % 4) * 4 + (y + k % 4) % 4

    def s3_copy(k, slot):
        return remote(
            piv_ref.at[slot], piv_ref.at[slot], s3_send.at[k], s3_recv.at[slot], r, peer(k)
        )

    loop(1, N_COL, lambda k: s3_copy(k, c).start())

    def z_copy(k, slot):
        return remote(
            zbuf.at[slot], zbuf.at[slot], z_send.at[k], z_recv.at[slot],
            ((z + k) % 4) * 2 + core, c,
        )

    loop(1, 4, lambda k: z_copy(k, z).start())

    def second_go(i):
        def go(k):
            top_along_y(i, k).start()
            low_along_x(i, k).start()

        loop(1, 4, go)

    second_go(0)
    for i in (1, 3, 2):
        remote(top(x_at(i)), top(x_at(i)), p1_send.at[0], h0_recv.at[x_at(i)], r, c).wait_recv()
        remote(low(y_at(i)), low(y_at(i)), p1_send.at[0], h1_recv.at[y_at(i)], r, c).wait_recv()
        second_go(i)

    loop(1, N_COL, lambda k: s3_copy(k, peer(k)).wait_recv())

    signal = signal_ref[0, 0]
    scale = lax.rsqrt(scale_ref[...]) * FOLD
    pivots = jnp.concatenate([piv_ref[p, 0:16, :] for p in range(16)], axis=0) * scale
    u2 = mm(left_operand(pivots), right_operand(pivots.T))
    row_id = lax.broadcasted_iota(jnp.int32, (B, B), 0)
    col_id = lax.broadcasted_iota(jnp.int32, (B, B), 1)
    noise = pivot_noise(piv_ref[0, 16:PIECE, :], piv_ref[12, 16:PIECE, :])
    aug[:, 0:B] = matern(u2, signal) + jnp.where(row_id == col_id, noise, 0.0)
    aug[:, B:2 * B] = jnp.where(row_id == col_id, 1.0, 0.0)

    to_row = 2 * z + index % 2

    def xy_each(k, act):
        source = (z + k) % 4
        target = 2 * (2 * source + core) + c // 8
        mine = (target == c) & (to_row == r)

        @pl.when(mine)
        def _():
            act(None, pltpu.make_async_copy(zbuf.at[source], cols_ref.at[index], cols_recv.at[index]))

        @pl.when(jnp.logical_not(mine))
        def _():
            act(
                remote(
                    zbuf.at[source], cols_ref.at[index], xy_send.at[k], cols_recv.at[index],
                    to_row, target,
                ),
                None,
            )

    def start_either(far, near):
        (far or near).start()

    def wait_far(far, near):
        if far is not None:
            far.wait_send()

    xy_each(0, start_either)

    def z_then_xy(k):
        slot = (z + k) % 4
        z_copy(k, slot).wait_recv()
        xy_each(k, start_either)

    loop(1, 4, z_then_xy)

    def sib_copy(i):
        return remote(cols_ref.at[i], cols_ref.at[i], sib_send.at[i], cols_recv.at[i], sib, c)

    def wait_cols(i):
        pltpu.make_async_copy(zbuf.at[0], cols_ref.at[i], cols_recv.at[i]).wait()

    def hand_over(k):
        i = 2 * k + core
        wait_cols(i)
        sib_copy(i).start()

    def between(step):
        @pl.when(step == B // NB - 1)
        def _():
            loop(0, 4, hand_over)

    eliminate(aug, w_ref, between)

    loop(0, 4, lambda k: wait_cols(2 * k + 1 - core))

    def rows_wait(i):
        def each(j):
            slot = x_at(i) // 4 * 4 + y_at(j) % 4

            @pl.when(j > 0)
            def _():
                remote(top(slot), top(slot), p1_send.at[0], h0_recv.at[slot], r, c).wait_recv()

            @pl.when(i > 0)
            def _():
                remote(low(slot), low(slot), p1_send.at[0], h1_recv.at[slot], r, c).wait_recv()

        loop(0, 4, each)

    loop(0, 4, rows_wait)

    def second_sent(i):
        def each(k):
            top_along_y(i, k).wait_send()
            low_along_x(i, k).wait_send()

        loop(1, 4, each)

    loop(0, 4, second_sent)

    def first_sent(k):
        top_along_x(k).wait_send()
        low_along_y(k).wait_send()
        z_copy(k, z).wait_send()

    loop(1, 4, first_sent)
    loop(1, N_COL, lambda k: s3_copy(k, c).wait_send())
    loop(0, 4, lambda k: xy_each(k, wait_far))
    loop(0, 4, lambda k: sib_copy(2 * k + core).wait_send())

    @pl.when((r == 0) & (c == 0))
    def _():
        loop(1, 12, lambda q: s1_copy(q, q).wait_send())

    @pl.when((r == 0) & (c == 1))
    def _():
        loop(0, 4, lambda q: s1_copy(q, 12 + q).wait_send())

    @pl.when(r == 0)
    def _():
        loop(1, N_ROW, lambda k: s2_copy(k).wait_send())


def gather(features, noise, scales, signal):
    vmem = pl.BlockSpec(memory_space=pltpu.VMEM)
    smem = pl.BlockSpec(memory_space=pltpu.SMEM)
    hbm = pl.BlockSpec(memory_space=pltpu.HBM)
    dma = pltpu.SemaphoreType.DMA
    return pl.pallas_call(
        gather_kernel,
        out_shape=(
            jax.ShapeDtypeStruct((N_COL, OWN, F), F32),
            jax.ShapeDtypeStruct((8, BLOCK, F), F32),
            jax.ShapeDtypeStruct((16, PIECE, F), F32),
            jax.ShapeDtypeStruct((B, B), F32),
        ),
        in_specs=[hbm, hbm, hbm, smem],
        out_specs=(vmem,) * 4,
        scratch_shapes=[
            pltpu.VMEM((12, PIECE, F), F32),
            pltpu.VMEM((4, BLOCK, F), F32),
            pltpu.VMEM((B, 2 * B), F32),
            pltpu.VMEM((1, OWN), F32),
            pltpu.VMEM((1, F), F32),
            dma((4,)), dma((12,)), dma, dma((8,)), dma, dma((16,)), dma((16,)),
            dma((8,)), dma((16,)), dma((16,)), dma((16,)), dma((16,)),
            dma((4,)), dma((4,)), dma((4,)), dma((8,)), dma((8,)),
        ],
        compiler_params=pltpu.CompilerParams(
            collective_id=0, has_side_effects=True, vmem_limit_bytes=32 * 1024 * 1024
        ),
        cost_estimate=pl.CostEstimate(flops=10**8, bytes_accessed=10**7, transcendentals=0),
    )(features, noise, scales, signal)


def update_kernel(
    rows_ref, cols_ref, piv_ref, w_ref, scale_ref, signal_ref,
    out_hbm, panel_hbm,
    right_d, right_p, right_piv, right_w, left_d, left_p, outs, panels, out_sem, panel_sem,
):
    r = lax.axis_index("row")
    c = lax.axis_index("col")
    signal = signal_ref[0, 0]
    scale = lax.rsqrt(scale_ref[...]) * FOLD
    noise = pivot_noise(piv_ref[0, 16:PIECE, :], piv_ref[12, 16:PIECE, :])

    def pair(ref, at):
        return jnp.concatenate([ref[at, 0:OWN, :], ref[at + 1, 0:OWN, :]], axis=0) * scale

    pivots = jnp.concatenate([piv_ref[p, 0:16, :] for p in range(16)], axis=0) * scale
    right_piv[...] = right_operand(pivots.T)
    left = left_operand(pivots)
    for i in range(4):
        right_d[:, TILE * i:TILE * (i + 1)] = right_operand(pair(cols_ref, 2 * i).T)
    w = w_ref[...]
    w_high, w_low = split2(w)
    wt_high, wt_low = split2(w.T)
    right_w[...] = jnp.concatenate([wt_high, wt_high, wt_low], axis=0)
    w3 = jnp.concatenate([w_high, w_low, w_high], axis=1)
    k_pc = matern(mm(left, right_d[...]), signal)
    row_id = lax.broadcasted_iota(jnp.int32, (B, COLS), 0)
    col_id = lax.broadcasted_iota(jnp.int32, (B, COLS), 1)
    line = jnp.concatenate([noise] * 6, axis=1)
    k_pc = k_pc + jnp.where((row_id == col_id) & (c == 0), line, 0.0)
    k_high, k_low = split2(k_pc)
    p_high, p_low = split2(mm(w3, jnp.concatenate([k_high, k_high, k_low], axis=0)))
    right_p[...] = jnp.concatenate([p_high, p_high, p_low], axis=0)

    def rows_of(t):
        return pl.ds(pl.multiple_of(t * TILE, TILE), TILE)

    def panel_copy(t):
        return pltpu.make_async_copy(panels.at[rows_of(t), :], panel_hbm.at[rows_of(t), :], panel_sem.at[t])

    def front(t):
        scaled = left_operand(pair(rows_ref, 2 * t))
        left_d[rows_of(t), :] = scaled
        k_rp = matern(mm(scaled, right_piv[...]), signal)
        row_id = lax.broadcasted_iota(jnp.int32, (TILE, B), 0)
        col_id = lax.broadcasted_iota(jnp.int32, (TILE, B), 1)
        k_rp = k_rp + jnp.where((row_id == col_id) & (t == 0) & (r == 0), noise, 0.0)
        k_high, k_low = split2(k_rp)
        panel = mm(jnp.concatenate([k_high, k_low, k_high], axis=1), right_w[...])
        panels[rows_of(t), :] = panel
        p_high, p_low = split2(-panel)
        left_p[rows_of(t), :] = jnp.concatenate([p_high, p_low, p_high], axis=1)
        panel_copy(t).start()

    def out_copy(t, slot):
        return pltpu.make_async_copy(outs.at[slot], out_hbm.at[rows_of(t), :], out_sem.at[slot])

    loop(0, STEPS, front)

    def main(t):
        slot = t % 2

        @pl.when(t >= 2)
        def _():
            out_copy(t - 2, slot).wait()

        outs[slot] = matern(mm(left_d[rows_of(t), :], right_d[...]), signal) + mm(
            left_p[rows_of(t), :], right_p[...]
        )

        first = t - (c % 2) * 4

        @pl.when((r == c // 2) & (first >= 0) & (first < 4))
        def _():
            at = pl.multiple_of(first * TILE, TILE)
            lines = []
            for k in range(2):
                tile = cols_ref[2 * first + k, OWN:BLOCK, :]
                lines += [tile[0:1, :], tile[1:2, 0:64]]
            line = jnp.concatenate(lines, axis=1)
            row_id = lax.broadcasted_iota(jnp.int32, (TILE, TILE), 0)
            col_id = lax.broadcasted_iota(jnp.int32, (TILE, TILE), 1)
            outs[slot, :, pl.ds(at, TILE)] += jnp.where(row_id == col_id, line, 0.0)

        out_copy(t, slot).start()

    loop(0, STEPS, main)
    loop(0, STEPS, lambda t: panel_copy(t).wait())
    out_copy(STEPS - 2, 0).wait()
    out_copy(STEPS - 1, 1).wait()


def update(rows, cols, piv, w, scales, signal):
    vmem = pl.BlockSpec(memory_space=pltpu.VMEM)
    smem = pl.BlockSpec(memory_space=pltpu.SMEM)
    hbm = pl.BlockSpec(memory_space=pltpu.HBM)
    dma = pltpu.SemaphoreType.DMA
    return pl.pallas_call(
        update_kernel,
        out_shape=(
            jax.ShapeDtypeStruct((N_COL * OWN, COLS), F32),
            jax.ShapeDtypeStruct((N_COL * OWN, B), F32),
        ),
        in_specs=[vmem, vmem, vmem, vmem, vmem, smem],
        out_specs=(hbm, hbm),
        scratch_shapes=[
            pltpu.VMEM((4 * F, COLS), BF16),
            pltpu.VMEM((3 * B, COLS), BF16),
            pltpu.VMEM((4 * F, B), BF16),
            pltpu.VMEM((3 * B, B), BF16),
            pltpu.VMEM((N_COL * OWN, 4 * F), BF16),
            pltpu.VMEM((N_COL * OWN, 3 * B), BF16),
            pltpu.VMEM((2, TILE, COLS), F32),
            pltpu.VMEM((N_COL * OWN, B), F32),
            dma((2,)), dma((STEPS,)),
        ],
        compiler_params=pltpu.CompilerParams(vmem_limit_bytes=48 * 1024 * 1024),
        cost_estimate=pl.CostEstimate(flops=12 * 10**9, bytes_accessed=25 * 10**6, transcendentals=10**7),
    )(rows, cols, piv, w, scales, signal)


def local(features, squared_scales, noise_var, signal):
    scales = squared_scales.reshape(1, F)
    signal = signal.reshape(1, 1)
    rows, cols, piv, w = gather(features, noise_var.reshape(1, OWN), scales, signal)
    return update(rows, cols, piv, w, scales, signal)


def solution(mesh):
    return jax.shard_map(
        local,
        mesh=mesh,
        in_specs=(P(("row", "col"), None), P(), P(("row", "col")), P()),
        out_specs=(P("row", "col"), P("row", None)),
        check_vma=False,
    )
```

```python
import functools
import math

import jax
import jax.numpy as jnp
from jax import lax
from jax.experimental import pallas as pl
from jax.experimental.pallas import tpu as pltpu
from jax.sharding import PartitionSpec as P

MESH = pl.DeviceIdType.MESH
F = 128
B = 256
OWN = 192
BLOCK = 200
PIECE = 24
N_ROW = 8
N_COL = 16
NB = 32
TILE = 384
STEPS = 8
COLS = 1536
HALF = 96
CHUNK = 512
SPANS = ((0, 512), (512, 1024), (1024, 1536), (1536, 1792))
FOLD = math.sqrt(5.0) / math.log(2.0)
LN2 = math.log(2.0)
BF16 = jnp.bfloat16
F32 = jnp.float32


def split2(a):
    high = a.astype(BF16)
    return high, (a - high.astype(F32)).astype(BF16)


def split3(a):
    high = a.astype(BF16)
    rest = a - high.astype(F32)
    mid = rest.astype(BF16)
    return high, mid, (rest - mid.astype(F32)).astype(BF16)


def mm(a, b):
    return jnp.dot(a, b, preferred_element_type=F32)


def left_parts(scaled):
    high, low = split2(scaled)
    return high, low, 0.25 * jnp.sum(scaled * scaled, axis=1, keepdims=True)


def left_ones(n):
    return jnp.where(lax.broadcasted_iota(jnp.int32, (n, F), 1) < 3, 1.0, 0.0).astype(BF16)


def right_operand(scaled_t):
    n = scaled_t.shape[1]
    sq = -jnp.sum(scaled_t * scaled_t, axis=0, keepdims=True)
    high, low = split2(scaled_t)
    one, two, three = (part.astype(F32) for part in split3(sq))
    sub = lax.broadcasted_iota(jnp.int32, (16, n), 0)
    extra = jnp.where(sub == 0, one, jnp.where(sub == 1, two, jnp.where(sub == 2, three, 0.0)))
    return jnp.concatenate(
        [high, high, low, extra.astype(BF16), jnp.zeros((F - 16, n), BF16)], axis=0
    )


def kernel_values(scaled2, right, signal):
    high, low, sq = left_parts(scaled2)
    left = jnp.concatenate([high, low, high, left_ones(scaled2.shape[0])], axis=1)
    return matern(sq - mm(left, right), signal)


def eye(n):
    return lax.broadcasted_iota(jnp.int32, (n, n), 0) == lax.broadcasted_iota(jnp.int32, (n, n), 1)


def rows_of(t):
    return pl.ds(pl.multiple_of(t * TILE, TILE), TILE)


def matern(u2, signal):
    a = jnp.maximum(u2, 1e-30)
    u = a * lax.rsqrt(a)
    poly = signal + u * (signal * LN2 + u * (signal * (LN2 * LN2 / 3.0)))
    return poly * jnp.exp2(-u)


def pivot_noise(tile0, tile1):
    first = tile0[0:1, :]
    second = jnp.concatenate([tile0[1:2, 0:64], tile1[0:1, 0:64]], axis=1)
    return jnp.concatenate([first, second], axis=1)


def remote(src, dst, send, recv, rr, cc):
    return pltpu.make_async_remote_copy(
        src_ref=src, dst_ref=dst, send_sem=send, recv_sem=recv,
        device_id=(rr, cc), device_id_type=MESH,
    )


def loop(low, high, body):
    def step(k, carry):
        body(k)
        return carry

    lax.fori_loop(low, high, step, 0)


def eliminate(aug, w_ref, between):
    sub8 = lax.broadcasted_iota(jnp.int32, (8, F), 0)

    def block_step(step):
        between(step)
        base = pl.multiple_of(step * NB, NB)
        half = step // 4
        shift = lax.rem(F - NB * lax.rem(step, 4), F)
        group = aug[pl.ds(base, NB), pl.ds(pl.multiple_of(half * F, F), F)]
        group = pltpu.roll(group, shift, 1)
        rep = [
            [
                jnp.broadcast_to(group[8 * g:8 * g + 8, i:i + 1], (8, F)) if g >= i // 8 else None
                for g in range(4)
            ]
            for i in range(NB)
        ]
        panel = [aug[pl.ds(base + 8 * g, 8), :] for g in range(4)]
        root = []
        for j in range(NB):
            gj, sj = divmod(j, 8)
            pivot = jnp.broadcast_to(rep[j][gj][sj:sj + 1, :], (8, F))
            inverse = 1.0 / pivot
            root.append(lax.rsqrt(pivot))
            mult = [rep[j][g] * inverse if g >= gj else None for g in range(4)]
            for i in range(j + 1, NB):
                gi, si = divmod(i, 8)
                entry = jnp.broadcast_to(rep[j][gi][si:si + 1, :], (8, F))
                for g in range(gi, 4):
                    rep[i][g] = rep[i][g] - entry * mult[g]
            line = jnp.broadcast_to(panel[gj][sj:sj + 1, :], (8, 2 * B))
            for g in range(gj, 4):
                factor = mult[g]
                if g == gj:
                    factor = jnp.where(sub8 > sj, factor, 0.0)
                panel[g] = panel[g] - jnp.concatenate([factor] * 4, axis=1) * line
        out = []
        for g in range(4):
            scale_rows = root[8 * g]
            for s in range(1, 8):
                scale_rows = jnp.where(sub8 == s, root[8 * g + s], scale_rows)
            out.append(panel[g] * jnp.concatenate([scale_rows] * 4, axis=1))
        block = jnp.concatenate(out, axis=0)
        w_ref[pl.ds(base, NB), :] = block[:, B:2 * B]
        aug[...] -= jnp.dot(
            block[:, 0:B].T, block, precision=lax.Precision.HIGHEST, preferred_element_type=F32
        )

    loop(0, B // NB, block_step)


def build_kernel(
    feat_hbm, noise_hbm, scale_hbm, signal_ref,
    k_ref, k_pc_ref, w_ref,
    rows_ref, cols_ref, piv_ref, stage, tail, zbuf, aug, noise_ref, scale_ref,
    right_d, left_d,
    in_sem, s1_send, s1_recv, s2_send, s2_recv, s3_send, s3_recv, tail_send, tail_recv,
    w1_send, w1_recv, w2_send, w2_recv, w3_send, w3_recv,
    p1_send, h0_send, h1_send, h0_recv, h1_recv,
    z_send, z_recv, xy_send, cols_recv, sib_send,
):
    r = lax.axis_index("row")
    c = lax.axis_index("col")
    z = r // 2
    core = r % 2
    x = c // 4
    y = c % 4
    sib = z * 2 + (1 - core)
    index = c % 8
    root = (r == 0) & (c == 0)

    in_copies = (
        pltpu.make_async_copy(feat_hbm, zbuf.at[z, pl.ds(0, OWN), :], in_sem.at[0]),
        pltpu.make_async_copy(feat_hbm, rows_ref.at[c], in_sem.at[1]),
        pltpu.make_async_copy(noise_hbm, noise_ref, in_sem.at[2]),
        pltpu.make_async_copy(scale_hbm, scale_ref, in_sem.at[3]),
    )
    for copy in in_copies:
        copy.start()

    barrier = pltpu.get_barrier_semaphore()

    def signal_to(rr, cc):
        pl.semaphore_signal(barrier, inc=1, device_id=(rr, cc), device_id_type=MESH)

    def greet_z(k):
        signal_to(((z + k) % 4) * 2, c)
        signal_to(((z + k) % 4) * 2 + 1, c)

    loop(1, N_COL, lambda k: signal_to(r, (c + k) % N_COL))
    loop(1, 4, greet_z)
    loop(0, N_COL, lambda k: signal_to(sib, (c + k) % N_COL))

    for copy in in_copies:
        copy.wait()
    zbuf[z, OWN:BLOCK, :] = jnp.zeros((BLOCK - OWN, F), F32)
    zbuf[z, OWN:OWN + 1, :] = noise_ref[0:1, 0:F]
    zbuf[z, OWN + 1:OWN + 2, 0:64] = noise_ref[0:1, F:OWN]

    @pl.when((r == 0) & (c < 2))
    def _():
        tile = zbuf[z, OWN:BLOCK, :]
        for q in range(12):
            stage[q, 0:16, :] = zbuf[z, 16 * q:16 * q + 16, :]
            stage[q, 16:PIECE, :] = tile

    pl.semaphore_wait(barrier, 15 + 16 + 6)

    tail_copy = remote(stage.at[pl.ds(0, 4)], tail, tail_send, tail_recv, 0, 0)

    def s1_copy(q, target):
        return remote(stage.at[q], piv_ref.at[target], s1_send.at[q], s1_recv, 0, target)

    @pl.when(root)
    def _():
        loop(1, 12, lambda q: s1_copy(q, q).start())
        piv_ref[0] = stage[0]

    @pl.when((r == 0) & (c == 1))
    def _():
        tail_copy.start()
        loop(0, 4, lambda q: s1_copy(q, 12 + q).start())

    def x_at(k):
        return ((x + k) % 4) * 4 + y

    def y_at(k):
        return x * 4 + (y + k) % 4

    def top(slot):
        return rows_ref.at[slot, pl.ds(0, HALF), :]

    def bottom(slot):
        return rows_ref.at[slot, pl.ds(HALF, HALF), :]

    def top_along_x(k):
        return remote(top(c), top(c), p1_send.at[k], h0_recv.at[c], r, x_at(k))

    def bottom_along_y(k):
        return remote(bottom(c), bottom(c), p1_send.at[4 + k], h1_recv.at[c], r, y_at(k))

    def top_along_y(i, k):
        slot = x_at(i)
        return remote(top(slot), top(slot), h0_send.at[4 * i + k], h0_recv.at[slot], r, y_at(k))

    def bottom_along_x(i, k):
        slot = y_at(i)
        return remote(bottom(slot), bottom(slot), h1_send.at[4 * i + k], h1_recv.at[slot], r, x_at(k))

    def wait_top(slot):
        remote(top(slot), top(slot), p1_send.at[0], h0_recv.at[slot], r, c).wait_recv()

    def wait_bottom(slot):
        remote(bottom(slot), bottom(slot), p1_send.at[0], h1_recv.at[slot], r, c).wait_recv()

    def z_copy(k, slot):
        return remote(
            zbuf.at[slot], zbuf.at[slot], z_send.at[k], z_recv.at[slot],
            ((z + k) % 4) * 2 + core, c,
        )

    to_row = 2 * z + index % 2

    def xy_each(k, act_near, act_far):
        source = (z + k) % 4
        target = 2 * (2 * source + core) + c // 8
        mine = (target == c) & (to_row == r)

        @pl.when(mine)
        def _():
            act_near(zbuf.at[source], cols_ref.at[index], cols_recv.at[index])

        @pl.when(jnp.logical_not(mine))
        def _():
            act_far(
                remote(
                    zbuf.at[source], cols_ref.at[index], xy_send.at[k], cols_recv.at[index],
                    to_row, target,
                )
            )

    def xy_go(k):
        xy_each(
            k,
            lambda src, dst, sem: pltpu.make_async_copy(src, dst, sem).start(),
            lambda copy: copy.start(),
        )

    def first_go(k):
        top_along_x(k).start()
        bottom_along_y(k).start()

    def second_go(i):
        def go(k):
            top_along_y(i, k).start()
            bottom_along_x(i, k).start()

        loop(1, 4, go)

    loop(1, 4, first_go)
    loop(1, 4, lambda k: z_copy(k, z).start())
    xy_go(0)
    second_go(0)
    for i in (1, 3, 2):
        wait_top(x_at(i))
        wait_bottom(y_at(i))
        second_go(i)

    def s2_copy(k):
        return remote(piv_ref.at[c], piv_ref.at[c], s2_send.at[k], s2_recv, k, c)

    @pl.when((r == 0) & (c != 0))
    def _():
        s1_copy(0, c).wait_recv()

    @pl.when(r == 0)
    def _():
        loop(1, N_ROW, lambda k: s2_copy(k).start())

    def z_then_xy(k):
        z_copy(k, (z + k) % 4).wait_recv()
        xy_go(k)

    loop(1, 4, z_then_xy)

    @pl.when(r != 0)
    def _():
        s2_copy(0).wait_recv()

    def peer(k):
        return ((x + k // 4) % 4) * 4 + (y + k % 4) % 4

    def s3_copy(k, slot):
        return remote(
            piv_ref.at[slot], piv_ref.at[slot], s3_send.at[k], s3_recv.at[slot], r, peer(k)
        )

    loop(1, N_COL, lambda k: s3_copy(k, c).start())

    def sib_copy(i):
        return remote(cols_ref.at[i], cols_ref.at[i], sib_send.at[i], cols_recv.at[i], sib, c)

    def wait_cols(i):
        pltpu.make_async_copy(zbuf.at[0], cols_ref.at[i], cols_recv.at[i]).wait()

    def hand_over(k):
        i = 2 * k + core
        wait_cols(i)
        sib_copy(i).start()

    def w_piece(p):
        return w_ref.at[pl.ds(pl.multiple_of(16 * p, 16), 16), :]

    def w1_copy(p):
        return remote(w_piece(p), w_piece(p), w1_send.at[p], w1_recv, 0, p)

    def w2_copy(k):
        return remote(w_piece(c), w_piece(c), w2_send.at[k], w2_recv, k, c)

    def w3_copy(k, p):
        return remote(w_piece(p), w_piece(p), w3_send.at[k], w3_recv.at[p], r, peer(k))

    def w3_each(k, act):
        @pl.when((r != 0) | (peer(k) != 0))
        def _():
            act(w3_copy(k, c))

    def w3_go(k):
        w3_each(k, lambda copy: copy.start())

    signal = signal_ref[0, 0]
    scale = lax.rsqrt(scale_ref[...]) * FOLD

    @pl.when(root)
    def _():
        tail_copy.wait_recv()
        pivots = jnp.concatenate(
            [zbuf[0, 0:OWN, :]] + [tail[q, 0:16, :] for q in range(4)], axis=0
        ) * scale
        diagonal = pivot_noise(stage[0, 16:PIECE, :], tail[0, 16:PIECE, :])
        block = kernel_values(2.0 * pivots, right_operand(pivots.T), signal)
        aug[:, 0:B] = block + jnp.where(eye(B), diagonal, 0.0)
        aug[:, B:2 * B] = jnp.where(eye(B), 1.0, 0.0)

        def between(step):
            @pl.when(step == 5)
            def _():
                loop(0, 4, hand_over)

        eliminate(aug, w_ref, between)
        loop(1, N_COL, lambda p: w1_copy(p).start())

    @pl.when(jnp.logical_not(root))
    def _():
        loop(0, 4, hand_over)

    loop(1, N_COL, lambda k: s3_copy(k, peer(k)).wait_recv())
    loop(0, 4, lambda k: wait_cols(2 * k + 1 - core))

    pivots = jnp.concatenate([piv_ref[p, 0:16, :] for p in range(16)], axis=0) * scale
    noise = pivot_noise(piv_ref[0, 16:PIECE, :], piv_ref[12, 16:PIECE, :])
    right_d[:, COLS:COLS + B] = right_operand(pivots.T)
    for i in range(4):
        pair = jnp.concatenate([cols_ref[2 * i, 0:OWN, :], cols_ref[2 * i + 1, 0:OWN, :]], axis=0)
        right_d[:, TILE * i:TILE * (i + 1)] = right_operand((pair * scale).T)
    k_pc_ref[...] = kernel_values(2.0 * pivots, right_d[:, 0:COLS], signal)

    @pl.when(c == 0)
    def _():
        k_pc_ref[:, 0:B] += jnp.where(eye(B), noise, 0.0)

    left_d[:, 3 * F:4 * F] = left_ones(TILE)

    def tile(k):
        t = (c // 2 + k) % STEPS

        @pl.when((k == 2) & (r == 0))
        def _():
            @pl.when(c != 0)
            def _():
                w1_copy(c).wait_recv()

            loop(1, N_ROW, lambda to: w2_copy(to).start())
            loop(1, N_COL, w3_go)

        @pl.when((k == 4) & (r != 0))
        def _():
            w2_copy(0).wait_recv()
            loop(1, N_COL, w3_go)

        for m in range(2):
            slot = 2 * t + m

            @pl.when(slot % 4 != y)
            def _():
                wait_top(slot)

            @pl.when(slot // 4 != x)
            def _():
                wait_bottom(slot)

        pair = jnp.concatenate([rows_ref[2 * t], rows_ref[2 * t + 1]], axis=0)
        high, low, sq = left_parts(pair * (scale * 2.0))
        left_d[:, 0:F] = high
        left_d[:, F:2 * F] = low
        left_d[:, 2 * F:3 * F] = high
        for low_at, high_at in SPANS:
            u2 = sq - mm(left_d[...], right_d[:, low_at:high_at])
            k_ref[rows_of(t), low_at:high_at] = matern(u2, signal)

        first = t - (c % 2) * 4

        @pl.when((r == c // 2) & (first >= 0) & (first < 4))
        def _():
            at = pl.multiple_of(first * TILE, TILE)
            lines = []
            for m in range(2):
                noise_tile = cols_ref[2 * first + m, OWN:BLOCK, :]
                lines += [noise_tile[0:1, :], noise_tile[1:2, 0:64]]
            line = jnp.concatenate(lines, axis=1)
            k_ref[rows_of(t), pl.ds(at, TILE)] += jnp.where(eye(TILE), line, 0.0)

    loop(0, STEPS, tile)

    @pl.when(r == 0)
    def _():
        k_ref[0:B, COLS:COLS + B] += jnp.where(eye(B), noise, 0.0)

    @pl.when(jnp.logical_not(root))
    def _():
        loop(1, N_COL, lambda k: w3_copy(k, peer(k)).wait_recv())

    loop(1, N_COL, lambda k: w3_each(k, lambda copy: copy.wait_send()))

    def second_sent(i):
        def each(k):
            top_along_y(i, k).wait_send()
            bottom_along_x(i, k).wait_send()

        loop(1, 4, each)

    loop(0, 4, second_sent)

    def first_sent(k):
        top_along_x(k).wait_send()
        bottom_along_y(k).wait_send()
        z_copy(k, z).wait_send()

    loop(1, 4, first_sent)
    loop(1, N_COL, lambda k: s3_copy(k, c).wait_send())
    loop(0, 4, lambda k: xy_each(k, lambda src, dst, sem: None, lambda copy: copy.wait_send()))
    loop(0, 4, lambda k: sib_copy(2 * k + core).wait_send())

    @pl.when(root)
    def _():
        loop(1, 12, lambda q: s1_copy(q, q).wait_send())
        loop(1, N_COL, lambda p: w1_copy(p).wait_send())

    @pl.when((r == 0) & (c == 1))
    def _():
        tail_copy.wait_send()
        loop(0, 4, lambda q: s1_copy(q, 12 + q).wait_send())

    @pl.when(r == 0)
    def _():
        loop(1, N_ROW, lambda k: s2_copy(k).wait_send())
        loop(1, N_ROW, lambda k: w2_copy(k).wait_send())


def build(features, noise, scales, signal):
    vmem = pl.BlockSpec(memory_space=pltpu.VMEM)
    smem = pl.BlockSpec(memory_space=pltpu.SMEM)
    hbm = pl.BlockSpec(memory_space=pltpu.HBM)
    dma = pltpu.SemaphoreType.DMA
    return pl.pallas_call(
        build_kernel,
        out_shape=(
            pltpu.VMEM((N_COL * OWN, COLS + B), F32),
            pltpu.VMEM((B, COLS), F32),
            jax.ShapeDtypeStruct((B, B), F32),
        ),
        in_specs=[hbm, hbm, hbm, smem],
        out_specs=(vmem,) * 3,
        scratch_shapes=[
            pltpu.VMEM((N_COL, OWN, F), F32),
            pltpu.VMEM((8, BLOCK, F), F32),
            pltpu.VMEM((16, PIECE, F), F32),
            pltpu.VMEM((12, PIECE, F), F32),
            pltpu.VMEM((4, PIECE, F), F32),
            pltpu.VMEM((4, BLOCK, F), F32),
            pltpu.VMEM((B, 2 * B), F32),
            pltpu.VMEM((1, OWN), F32),
            pltpu.VMEM((1, F), F32),
            pltpu.VMEM((4 * F, COLS + B), BF16),
            pltpu.VMEM((TILE, 4 * F), BF16),
            dma((4,)), dma((12,)), dma, dma((8,)), dma, dma((16,)), dma((16,)), dma, dma,
            dma((16,)), dma, dma((8,)), dma, dma((16,)), dma((16,)),
            dma((8,)), dma((16,)), dma((16,)), dma((16,)), dma((16,)),
            dma((4,)), dma((4,)), dma((4,)), dma((8,)), dma((8,)),
        ],
        compiler_params=pltpu.CompilerParams(
            collective_id=0, has_side_effects=True, vmem_limit_bytes=28 * 1024 * 1024
        ),
        cost_estimate=pl.CostEstimate(flops=10**9, bytes_accessed=10**7, transcendentals=0),
    )(features, noise, scales, signal)


def apply_kernel(
    k_ref, k_pc_ref, w_ref,
    out_hbm, panel_hbm,
    right_p, right_w, left_p, panels, outs,
    out_sem, panel_sem,
):
    w = w_ref[...]
    wt_high, wt_low = split2(w.T)
    right_w[...] = jnp.concatenate([wt_high, wt_high, wt_low], axis=0)

    w_high, w_low = split2(w)
    left_w = jnp.concatenate([w_high, w_low, w_high], axis=1)
    for i in range(COLS // CHUNK):
        span = slice(CHUNK * i, CHUNK * (i + 1))
        k_high, k_low = split2(k_pc_ref[:, span])
        p_high, p_low = split2(mm(left_w, jnp.concatenate([k_high, k_high, k_low], axis=0)))
        right_p[0:B, span] = p_high
        right_p[B:2 * B, span] = p_high
        right_p[2 * B:3 * B, span] = p_low

    def panel_copy(t):
        return pltpu.make_async_copy(
            panels.at[rows_of(t), :], panel_hbm.at[rows_of(t), :], panel_sem.at[t]
        )

    def panel_tile(t):
        k_high, k_low = split2(k_ref[rows_of(t), COLS:COLS + B])
        panel = mm(jnp.concatenate([k_high, k_low, k_high], axis=1), right_w[...])
        panels[rows_of(t), :] = panel
        p_high, p_low = split2(panel)
        left_p[rows_of(t), 0:B] = p_high
        left_p[rows_of(t), B:2 * B] = p_low
        left_p[rows_of(t), 2 * B:3 * B] = p_high
        panel_copy(t).start()

    loop(0, STEPS, panel_tile)

    def out_copy(t, slot, i):
        span = pl.ds(CHUNK * i, CHUNK)
        return pltpu.make_async_copy(
            outs.at[slot, :, span], out_hbm.at[rows_of(t), span], out_sem.at[slot, i]
        )

    def main(t):
        slot = t % 2
        for i in range(COLS // CHUNK):
            @pl.when(t >= 2)
            def _():
                out_copy(t - 2, slot, i).wait()

            span = slice(CHUNK * i, CHUNK * (i + 1))
            outs[slot, :, span] = k_ref[rows_of(t), span] - mm(left_p[rows_of(t), :], right_p[:, span])
            out_copy(t, slot, i).start()

    loop(0, STEPS, main)
    loop(0, STEPS, lambda t: panel_copy(t).wait())
    for t in (STEPS - 2, STEPS - 1):
        for i in range(COLS // CHUNK):
            out_copy(t, t % 2, i).wait()


def apply_panel(k, k_pc, w):
    vmem = pl.BlockSpec(memory_space=pltpu.VMEM)
    hbm = pl.BlockSpec(memory_space=pltpu.HBM)
    dma = pltpu.SemaphoreType.DMA
    n = N_COL * OWN
    return pl.pallas_call(
        apply_kernel,
        out_shape=(jax.ShapeDtypeStruct((n, COLS), F32), jax.ShapeDtypeStruct((n, B), F32)),
        in_specs=[vmem, vmem, vmem],
        out_specs=(hbm, hbm),
        scratch_shapes=[
            pltpu.VMEM((3 * B, COLS), BF16),
            pltpu.VMEM((3 * B, B), BF16),
            pltpu.VMEM((n, 3 * B), BF16),
            pltpu.VMEM((n, B), F32),
            pltpu.VMEM((2, TILE, COLS), F32),
            dma((2, COLS // CHUNK)), dma((STEPS,)),
        ],
        compiler_params=pltpu.CompilerParams(vmem_limit_bytes=28 * 1024 * 1024),
        cost_estimate=pl.CostEstimate(flops=8 * 10**9, bytes_accessed=25 * 10**6, transcendentals=0),
    )(k, k_pc, w)


def local(features, squared_scales, noise_var, signal):
    hbm = lambda a: pltpu.with_memory_space_constraint(a, pltpu.HBM)
    k, k_pc, w = build(
        hbm(features),
        hbm(noise_var.reshape(1, OWN)),
        hbm(squared_scales.reshape(1, F)),
        signal.reshape(1, 1),
    )
    return apply_panel(*(pltpu.with_memory_space_constraint(a, pltpu.VMEM) for a in (k, k_pc, w)))


def solution(mesh):
    return jax.shard_map(
        local,
        mesh=mesh,
        in_specs=(P(("row", "col"), None), P(), P(("row", "col")), P()),
        out_specs=(P("row", "col"), P("row", None)),
        check_vma=False,
    )
```

```python
import functools
import math

import jax
import jax.numpy as jnp
from jax import lax
from jax.experimental import pallas as pl
from jax.experimental.pallas import tpu as pltpu
from jax.sharding import PartitionSpec as P

MESH = pl.DeviceIdType.MESH
F = 128
B = 256
OWN = 192
BLOCK = 200
PIECE = 24
N_ROW = 8
N_COL = 16
NB = 32
TILE = 384
PT = 1536
PARTS = 1
MC = 512
STEPS = 8
COLS = 1536
HALF = 96
CHUNK = 512
W_AT = (1, 3)
SPANS = ((0, 512), (512, 1024), (1024, 1536), (1536, 1792))
FOLD = math.sqrt(5.0) / math.log(2.0)
LN2 = math.log(2.0)
BF16 = jnp.bfloat16
F32 = jnp.float32


def split2(a):
    high = a.astype(BF16)
    return high, (a - high.astype(F32)).astype(BF16)


def split3(a):
    high = a.astype(BF16)
    rest = a - high.astype(F32)
    mid = rest.astype(BF16)
    return high, mid, (rest - mid.astype(F32)).astype(BF16)


def mm(a, b):
    return jnp.dot(a, b, preferred_element_type=F32)


def left_parts(scaled):
    high, low = split2(scaled)
    return high, low, 0.25 * jnp.sum(scaled * scaled, axis=1, keepdims=True)


def left_ones(n):
    return jnp.where(lax.broadcasted_iota(jnp.int32, (n, F), 1) < 3, 1.0, 0.0).astype(BF16)


def right_operand(scaled_t):
    n = scaled_t.shape[1]
    sq = -jnp.sum(scaled_t * scaled_t, axis=0, keepdims=True)
    high, low = split2(scaled_t)
    one, two, three = (part.astype(F32) for part in split3(sq))
    sub = lax.broadcasted_iota(jnp.int32, (16, n), 0)
    extra = jnp.where(sub == 0, one, jnp.where(sub == 1, two, jnp.where(sub == 2, three, 0.0)))
    return jnp.concatenate(
        [high, high, low, extra.astype(BF16), jnp.zeros((F - 16, n), BF16)], axis=0
    )


def kernel_values(scaled2, right, signal):
    high, low, sq = left_parts(scaled2)
    left = jnp.concatenate([high, low, high, left_ones(scaled2.shape[0])], axis=1)
    return matern(sq - mm(left, right), signal)


def eye(n):
    return lax.broadcasted_iota(jnp.int32, (n, n), 0) == lax.broadcasted_iota(jnp.int32, (n, n), 1)


def rows_of(t):
    return pl.ds(pl.multiple_of(t * TILE, TILE), TILE)


def matern(u2, signal):
    start = jnp.log2(jnp.full((1, 1), LN2 * LN2 / 3.0, F32) * signal)
    a = jnp.maximum(u2, 1e-30)
    u = a * lax.rsqrt(a)
    v = u + 1.5 / LN2
    return (v * v + 0.75 / (LN2 * LN2)) * jnp.exp2(start - u)


def pivot_noise(tile0, tile1):
    first = tile0[0:1, :]
    second = jnp.concatenate([tile0[1:2, 0:64], tile1[0:1, 0:64]], axis=1)
    return jnp.concatenate([first, second], axis=1)


def remote(src, dst, send, recv, rr, cc):
    return pltpu.make_async_remote_copy(
        src_ref=src, dst_ref=dst, send_sem=send, recv_sem=recv,
        device_id=(rr, cc), device_id_type=MESH,
    )


def loop(low, high, body):
    def step(k, carry):
        body(k)
        return carry

    lax.fori_loop(low, high, step, 0)


def eliminate(aug, w_ref, between):
    sub8 = lax.broadcasted_iota(jnp.int32, (8, F), 0)

    def block_step(step, half):
        between(step)
        base = pl.multiple_of(step * NB, NB)
        shift = lax.rem(F - NB * lax.rem(step, 4), F)
        width = 3 * F
        span = slice(half * F, half * F + width)
        panel = [aug[pl.ds(base + 8 * g, 8), span] for g in range(4)]
        group = pltpu.roll(jnp.concatenate([part[:, 0:F] for part in panel], axis=0), shift, 1)
        rep = [
            [
                jnp.broadcast_to(group[8 * g:8 * g + 8, i:i + 1], (8, F)) if g >= i // 8 else None
                for g in range(4)
            ]
            for i in range(NB)
        ]
        root = []
        for j in range(NB):
            gj, sj = divmod(j, 8)
            pivot = jnp.broadcast_to(rep[j][gj][sj:sj + 1, :], (8, F))
            inverse = 1.0 / pivot
            root.append(lax.rsqrt(pivot))
            mult = [rep[j][g] * inverse if g >= gj else None for g in range(4)]
            for i in range(j + 1, NB):
                gi, si = divmod(i, 8)
                entry = jnp.broadcast_to(rep[j][gi][si:si + 1, :], (8, F))
                for g in range(gi, 4):
                    rep[i][g] = rep[i][g] - entry * mult[g]
            line = jnp.broadcast_to(panel[gj][sj:sj + 1, :], (8, width))
            for g in range(gj, 4):
                factor = mult[g]
                if g == gj:
                    factor = jnp.where(sub8 > sj, factor, 0.0)
                panel[g] = panel[g] - jnp.concatenate([factor] * 3, axis=1) * line
        out = []
        for g in range(4):
            scale_rows = root[8 * g]
            for s in range(1, 8):
                scale_rows = jnp.where(sub8 == s, root[8 * g + s], scale_rows)
            out.append(panel[g] * jnp.concatenate([scale_rows] * 3, axis=1))
        block = jnp.concatenate(out, axis=0)
        if half == 0:
            w_ref[pl.ds(base, NB), 0:F] = block[:, 2 * F:3 * F]
            w_ref[pl.ds(base, NB), F:B] = jnp.zeros((NB, F), F32)
            left = block[:, 0:B]
        else:
            w_ref[pl.ds(base, NB), :] = block[:, F:3 * F]
            left = block[:, 0:F]
        aug[half * F:B, span] -= jnp.dot(
            left.T, block, precision=lax.Precision.HIGHEST, preferred_element_type=F32
        )

    loop(0, 4, lambda step: block_step(step, 0))
    loop(4, 8, lambda step: block_step(step, 1))


def build_kernel(
    feat_hbm, noise_hbm, scale_hbm, signal_ref,
    k_ref, k_pc_ref, w_ref,
    rows_ref, cols_ref, piv_ref, stage, tail, zbuf, aug, noise_ref, scale_ref,
    right_d, left_d,
    in_sem, s1_send, s1_recv, s2_send, s2_recv, s3_send, s3_recv, tail_send, tail_recv,
    w1_send, w1_recv, w2_send, w2_recv, w3_send, w3_recv,
    p1_send, h0_send, h1_send, h0_recv, h1_recv,
    z_send, z_recv, xy_send, cols_recv, sib_send,
):
    r = lax.axis_index("row")
    c = lax.axis_index("col")
    z = r // 2
    core = r % 2
    x = c // 4
    y = c % 4
    sib = z * 2 + (1 - core)
    index = c % 8
    root = (r == 0) & (c == 0)

    in_copies = (
        pltpu.make_async_copy(feat_hbm, zbuf.at[z, pl.ds(0, OWN), :], in_sem.at[0]),
        pltpu.make_async_copy(feat_hbm, rows_ref.at[c], in_sem.at[1]),
        pltpu.make_async_copy(noise_hbm, noise_ref, in_sem.at[2]),
        pltpu.make_async_copy(scale_hbm, scale_ref, in_sem.at[3]),
    )
    for copy in in_copies:
        copy.start()

    barrier = pltpu.get_barrier_semaphore()

    def signal_to(rr, cc):
        pl.semaphore_signal(barrier, inc=1, device_id=(rr, cc), device_id_type=MESH)

    def greet_z(k):
        signal_to(((z + k) % 4) * 2, c)
        signal_to(((z + k) % 4) * 2 + 1, c)

    loop(1, N_COL, lambda k: signal_to(r, (c + k) % N_COL))
    loop(1, 4, greet_z)
    loop(0, N_COL, lambda k: signal_to(sib, (c + k) % N_COL))

    for copy in in_copies:
        copy.wait()
    zbuf[z, OWN:BLOCK, :] = jnp.zeros((BLOCK - OWN, F), F32)
    zbuf[z, OWN:OWN + 1, :] = noise_ref[0:1, 0:F]
    zbuf[z, OWN + 1:OWN + 2, 0:64] = noise_ref[0:1, F:OWN]

    @pl.when((r == 0) & (c < 2))
    def _():
        tile = zbuf[z, OWN:BLOCK, :]
        for q in range(12):
            stage[q, 0:16, :] = zbuf[z, 16 * q:16 * q + 16, :]
            stage[q, 16:PIECE, :] = tile

    pl.semaphore_wait(barrier, 15 + 16 + 6)

    tail_copy = remote(stage.at[pl.ds(0, 4)], tail, tail_send, tail_recv, 0, 0)

    def s1_copy(q, target):
        return remote(stage.at[q], piv_ref.at[target], s1_send.at[q], s1_recv, 0, target)

    @pl.when(root)
    def _():
        loop(1, 12, lambda q: s1_copy(q, q).start())
        piv_ref[0] = stage[0]

    @pl.when((r == 0) & (c == 1))
    def _():
        tail_copy.start()
        loop(0, 4, lambda q: s1_copy(q, 12 + q).start())

    def x_at(k):
        return ((x + k) % 4) * 4 + y

    def y_at(k):
        return x * 4 + (y + k) % 4

    def top(slot):
        return rows_ref.at[slot, pl.ds(0, HALF), :]

    def bottom(slot):
        return rows_ref.at[slot, pl.ds(HALF, HALF), :]

    def top_along_x(k):
        return remote(top(c), top(c), p1_send.at[k], h0_recv.at[c], r, x_at(k))

    def bottom_along_y(k):
        return remote(bottom(c), bottom(c), p1_send.at[4 + k], h1_recv.at[c], r, y_at(k))

    def top_along_y(i, k):
        slot = x_at(i)
        return remote(top(slot), top(slot), h0_send.at[4 * i + k], h0_recv.at[slot], r, y_at(k))

    def bottom_along_x(i, k):
        slot = y_at(i)
        return remote(bottom(slot), bottom(slot), h1_send.at[4 * i + k], h1_recv.at[slot], r, x_at(k))

    def wait_top(slot):
        remote(top(slot), top(slot), p1_send.at[0], h0_recv.at[slot], r, c).wait_recv()

    def wait_bottom(slot):
        remote(bottom(slot), bottom(slot), p1_send.at[0], h1_recv.at[slot], r, c).wait_recv()

    def z_copy(k, slot):
        return remote(
            zbuf.at[slot], zbuf.at[slot], z_send.at[k], z_recv.at[slot],
            ((z + k) % 4) * 2 + core, c,
        )

    to_row = 2 * z + index % 2

    def xy_each(k, act_near, act_far):
        source = (z + k) % 4
        target = 2 * (2 * source + core) + c // 8
        mine = (target == c) & (to_row == r)

        @pl.when(mine)
        def _():
            act_near(zbuf.at[source], cols_ref.at[index], cols_recv.at[index])

        @pl.when(jnp.logical_not(mine))
        def _():
            act_far(
                remote(
                    zbuf.at[source], cols_ref.at[index], xy_send.at[k], cols_recv.at[index],
                    to_row, target,
                )
            )

    def xy_go(k):
        xy_each(
            k,
            lambda src, dst, sem: pltpu.make_async_copy(src, dst, sem).start(),
            lambda copy: copy.start(),
        )

    def first_go(k):
        top_along_x(k).start()
        bottom_along_y(k).start()

    def second_go(i):
        def go(k):
            top_along_y(i, k).start()
            bottom_along_x(i, k).start()

        loop(1, 4, go)

    def rest_of_rows():
        for i in (1, 3, 2):
            wait_top(x_at(i))
            wait_bottom(y_at(i))
            second_go(i)

    def rest_of_columns():
        for k in (1, 3, 2):
            z_copy(k, (z + k) % 4).wait_recv()
            xy_go(k)

    loop(1, 4, lambda k: z_copy(k, z).start())
    loop(1, 4, first_go)
    xy_go(0)
    second_go(0)

    def s2_copy(k):
        return remote(piv_ref.at[c], piv_ref.at[c], s2_send.at[k], s2_recv, k, c)

    @pl.when((r == 0) & (c != 0))
    def _():
        s1_copy(0, c).wait_recv()

    @pl.when(r == 0)
    def _():
        loop(1, N_ROW, lambda k: s2_copy(k).start())

    def peer(k):
        return ((x + k // 4) % 4) * 4 + (y + k % 4) % 4

    def s3_copy(k, slot):
        return remote(
            piv_ref.at[slot], piv_ref.at[slot], s3_send.at[k], s3_recv.at[slot], r, peer(k)
        )

    @pl.when(r == 0)
    def _():
        loop(1, N_COL, lambda k: s3_copy(k, c).start())

    def sib_copy(i):
        return remote(cols_ref.at[i], cols_ref.at[i], sib_send.at[i], cols_recv.at[i], sib, c)

    def wait_cols(i):
        pltpu.make_async_copy(zbuf.at[0], cols_ref.at[i], cols_recv.at[i]).wait()

    def hand_over(k):
        i = 2 * k + core
        wait_cols(i)
        sib_copy(i).start()

    def w_piece(p):
        return w_ref.at[pl.ds(pl.multiple_of(16 * p, 16), 16), :]

    def w1_copy(p):
        return remote(w_piece(p), w_piece(p), w1_send.at[p], w1_recv, 0, p)

    def w2_copy(k):
        return remote(w_piece(c), w_piece(c), w2_send.at[k], w2_recv, k, c)

    def w3_copy(k, p):
        return remote(w_piece(p), w_piece(p), w3_send.at[k], w3_recv.at[p], r, peer(k))

    def w3_each(k, act):
        @pl.when((r != 0) | (peer(k) != 0))
        def _():
            act(w3_copy(k, c))

    def w3_go(k):
        w3_each(k, lambda copy: copy.start())

    signal = signal_ref[0, 0]
    scale = lax.rsqrt(scale_ref[...]) * FOLD

    @pl.when(root)
    def _():
        tail_copy.wait_recv()
        pivots = jnp.concatenate(
            [zbuf[0, 0:OWN, :]] + [tail[q, 0:16, :] for q in range(4)], axis=0
        ) * scale
        diagonal = pivot_noise(stage[0, 16:PIECE, :], tail[0, 16:PIECE, :])
        block = kernel_values(2.0 * pivots, right_operand(pivots.T), signal)
        aug[:, 0:B] = block + jnp.where(eye(B), diagonal, 0.0)
        aug[:, B:2 * B] = jnp.where(eye(B), 1.0, 0.0)

        def between(step):
            @pl.when(step == 2)
            def _():
                rest_of_columns()

            @pl.when(step == 5)
            def _():
                loop(0, 4, hand_over)
                rest_of_rows()

        eliminate(aug, w_ref, between)
        loop(1, N_COL, lambda p: w1_copy(p).start())

    @pl.when(jnp.logical_not(root))
    def _():
        rest_of_columns()

        @pl.when(r != 0)
        def _():
            s2_copy(0).wait_recv()
            loop(1, N_COL, lambda k: s3_copy(k, c).start())

        loop(0, 4, hand_over)
        rest_of_rows()

    loop(1, N_COL, lambda k: s3_copy(k, peer(k)).wait_recv())
    loop(0, 4, lambda k: wait_cols(2 * k + 1 - core))

    pivots = jnp.concatenate([piv_ref[p, 0:16, :] for p in range(16)], axis=0) * scale
    noise = pivot_noise(piv_ref[0, 16:PIECE, :], piv_ref[12, 16:PIECE, :])
    right_d[:, COLS:COLS + B] = right_operand(pivots.T)
    for i in range(4):
        pair = jnp.concatenate([cols_ref[2 * i, 0:OWN, :], cols_ref[2 * i + 1, 0:OWN, :]], axis=0)
        right_d[:, TILE * i:TILE * (i + 1)] = right_operand((pair * scale).T)
    k_pc_ref[...] = kernel_values(2.0 * pivots, right_d[:, 0:COLS], signal)

    @pl.when(c == 0)
    def _():
        k_pc_ref[:, 0:B] += jnp.where(eye(B), noise, 0.0)

    left_d[:, 3 * F:4 * F] = left_ones(TILE)

    def tile(k):
        turn = k // 2
        turn = turn + turn // 2 - 2 * (turn // 3)
        t = 2 * ((x + turn) % 4) + (y // 2 + k) % 2

        @pl.when((k == W_AT[0]) & (r == 0))
        def _():
            @pl.when(c != 0)
            def _():
                w1_copy(c).wait_recv()

            loop(1, N_ROW, lambda to: w2_copy(to).start())
            loop(1, N_COL, w3_go)

        @pl.when((k == W_AT[1]) & (r != 0))
        def _():
            w2_copy(0).wait_recv()
            loop(1, N_COL, w3_go)

        for m in range(2):
            slot = 2 * t + m

            @pl.when(slot % 4 != y)
            def _():
                wait_top(slot)

            @pl.when(slot // 4 != x)
            def _():
                wait_bottom(slot)

        pair = jnp.concatenate([rows_ref[2 * t], rows_ref[2 * t + 1]], axis=0)
        high, low, sq = left_parts(pair * (scale * 2.0))
        left_d[:, 0:F] = high
        left_d[:, F:2 * F] = low
        left_d[:, 2 * F:3 * F] = high
        for low_at, high_at in SPANS:
            u2 = sq - mm(left_d[...], right_d[:, low_at:high_at])
            k_ref[rows_of(t), low_at:high_at] = matern(u2, signal)

        first = t - (c % 2) * 4

        @pl.when((r == c // 2) & (first >= 0) & (first < 4))
        def _():
            at = pl.multiple_of(first * TILE, TILE)
            lines = []
            for m in range(2):
                noise_tile = cols_ref[2 * first + m, OWN:BLOCK, :]
                lines += [noise_tile[0:1, :], noise_tile[1:2, 0:64]]
            line = jnp.concatenate(lines, axis=1)
            k_ref[rows_of(t), pl.ds(at, TILE)] += jnp.where(eye(TILE), line, 0.0)

    loop(0, STEPS, tile)

    @pl.when(r == 0)
    def _():
        k_ref[0:B, COLS:COLS + B] += jnp.where(eye(B), noise, 0.0)

    @pl.when(jnp.logical_not(root))
    def _():
        loop(1, N_COL, lambda k: w3_copy(k, peer(k)).wait_recv())

    loop(1, N_COL, lambda k: w3_each(k, lambda copy: copy.wait_send()))

    def second_sent(i):
        def each(k):
            top_along_y(i, k).wait_send()
            bottom_along_x(i, k).wait_send()

        loop(1, 4, each)

    loop(0, 4, second_sent)

    def first_sent(k):
        top_along_x(k).wait_send()
        bottom_along_y(k).wait_send()
        z_copy(k, z).wait_send()

    loop(1, 4, first_sent)
    loop(1, N_COL, lambda k: s3_copy(k, c).wait_send())
    loop(0, 4, lambda k: xy_each(k, lambda src, dst, sem: None, lambda copy: copy.wait_send()))
    loop(0, 4, lambda k: sib_copy(2 * k + core).wait_send())

    @pl.when(root)
    def _():
        loop(1, 12, lambda q: s1_copy(q, q).wait_send())
        loop(1, N_COL, lambda p: w1_copy(p).wait_send())

    @pl.when((r == 0) & (c == 1))
    def _():
        tail_copy.wait_send()
        loop(0, 4, lambda q: s1_copy(q, 12 + q).wait_send())

    @pl.when(r == 0)
    def _():
        loop(1, N_ROW, lambda k: s2_copy(k).wait_send())
        loop(1, N_ROW, lambda k: w2_copy(k).wait_send())


def build(features, noise, scales, signal):
    vmem = pl.BlockSpec(memory_space=pltpu.VMEM)
    smem = pl.BlockSpec(memory_space=pltpu.SMEM)
    hbm = pl.BlockSpec(memory_space=pltpu.HBM)
    dma = pltpu.SemaphoreType.DMA
    return pl.pallas_call(
        build_kernel,
        out_shape=(
            pltpu.VMEM((N_COL * OWN, COLS + B), F32),
            pltpu.VMEM((B, COLS), F32),
            jax.ShapeDtypeStruct((B, B), F32),
        ),
        in_specs=[hbm, hbm, hbm, smem],
        out_specs=(vmem,) * 3,
        scratch_shapes=[
            pltpu.VMEM((N_COL, OWN, F), F32),
            pltpu.VMEM((8, BLOCK, F), F32),
            pltpu.VMEM((16, PIECE, F), F32),
            pltpu.VMEM((12, PIECE, F), F32),
            pltpu.VMEM((4, PIECE, F), F32),
            pltpu.VMEM((4, BLOCK, F), F32),
            pltpu.VMEM((B, 2 * B), F32),
            pltpu.VMEM((1, OWN), F32),
            pltpu.VMEM((1, F), F32),
            pltpu.VMEM((4 * F, COLS + B), BF16),
            pltpu.VMEM((TILE, 4 * F), BF16),
            dma((4,)), dma((12,)), dma, dma((8,)), dma, dma((16,)), dma((16,)), dma, dma,
            dma((16,)), dma, dma((8,)), dma, dma((16,)), dma((16,)),
            dma((8,)), dma((16,)), dma((16,)), dma((16,)), dma((16,)),
            dma((4,)), dma((4,)), dma((4,)), dma((8,)), dma((8,)),
        ],
        compiler_params=pltpu.CompilerParams(
            collective_id=0, has_side_effects=True, vmem_limit_bytes=28 * 1024 * 1024
        ),
        cost_estimate=pl.CostEstimate(flops=10**9, bytes_accessed=10**7, transcendentals=0),
    )(features, noise, scales, signal)


def apply_kernel(
    k_ref, k_pc_ref, w_ref,
    out_hbm, panel_hbm,
    right_p, right_w, left_p, panels, outs,
    out_sem, panel_sem,
):
    w = w_ref[...]
    wt_high, wt_low = split2(w.T)
    right_w[...] = jnp.concatenate([wt_high, wt_high, wt_low], axis=0)

    w_high, w_low = split2(w)
    left_w = jnp.concatenate([w_high, w_low, w_high], axis=1)
    for i in range(COLS // CHUNK):
        span = slice(CHUNK * i, CHUNK * (i + 1))
        k_high, k_low = split2(k_pc_ref[:, span])
        p_high, p_low = split2(mm(left_w, jnp.concatenate([k_high, k_high, k_low], axis=0)))
        right_p[0:B, span] = p_high
        right_p[B:2 * B, span] = p_high
        right_p[2 * B:3 * B, span] = p_low

    def prow(t):
        return pl.ds(pl.multiple_of(t * PT, PT), PT)

    def panel_copy(t):
        return pltpu.make_async_copy(
            panels.at[prow(t), :], panel_hbm.at[prow(t), :], panel_sem.at[t]
        )

    def panel_tile(t):
        k_high, k_low = split2(k_ref[prow(t), COLS:COLS + B])
        panel = mm(jnp.concatenate([k_high, k_low, k_high], axis=1), right_w[...])
        panels[prow(t), :] = panel
        p_high, p_low = split2(panel)
        left_p[prow(t), 0:B] = p_high
        left_p[prow(t), B:2 * B] = p_low
        left_p[prow(t), 2 * B:3 * B] = p_high
        panel_copy(t).start()

    loop(0, 3072 // PT, panel_tile)

    def out_copy(t, slot, i):
        part = TILE // PARTS
        rows = pl.ds(pl.multiple_of(t * TILE + part * i, 8), part)
        return pltpu.make_async_copy(
            outs.at[slot, pl.ds(part * i, part), :], out_hbm.at[rows, :], out_sem.at[slot, i]
        )

    def main(t):
        slot = t % 2

        @pl.when(t >= 2)
        def _():
            for i in range(PARTS):
                out_copy(t - 2, slot, i).wait()

        for i in range(COLS // MC):
            span = slice(MC * i, MC * (i + 1))
            outs[slot, :, span] = k_ref[rows_of(t), span] - mm(left_p[rows_of(t), :], right_p[:, span])
        for i in range(PARTS):
            out_copy(t, slot, i).start()

    loop(0, STEPS, main)
    loop(0, 3072 // PT, lambda t: panel_copy(t).wait())
    for t in (STEPS - 2, STEPS - 1):
        for i in range(PARTS):
            out_copy(t, t % 2, i).wait()


def apply_panel(k, k_pc, w):
    vmem = pl.BlockSpec(memory_space=pltpu.VMEM)
    hbm = pl.BlockSpec(memory_space=pltpu.HBM)
    dma = pltpu.SemaphoreType.DMA
    n = N_COL * OWN
    return pl.pallas_call(
        apply_kernel,
        out_shape=(jax.ShapeDtypeStruct((n, COLS), F32), jax.ShapeDtypeStruct((n, B), F32)),
        in_specs=[vmem, vmem, vmem],
        out_specs=(hbm, hbm),
        scratch_shapes=[
            pltpu.VMEM((3 * B, COLS), BF16),
            pltpu.VMEM((3 * B, B), BF16),
            pltpu.VMEM((n, 3 * B), BF16),
            pltpu.VMEM((n, B), F32),
            pltpu.VMEM((2, TILE, COLS), F32),
            dma((2, PARTS)), dma((STEPS,)),
        ],
        compiler_params=pltpu.CompilerParams(vmem_limit_bytes=28 * 1024 * 1024),
        cost_estimate=pl.CostEstimate(flops=8 * 10**9, bytes_accessed=25 * 10**6, transcendentals=0),
    )(k, k_pc, w)


def local(features, squared_scales, noise_var, signal):
    hbm = lambda a: pltpu.with_memory_space_constraint(a, pltpu.HBM)
    k, k_pc, w = build(
        hbm(features),
        hbm(noise_var.reshape(1, OWN)),
        hbm(squared_scales.reshape(1, F)),
        signal.reshape(1, 1),
    )
    return apply_panel(*(pltpu.with_memory_space_constraint(a, pltpu.VMEM) for a in (k, k_pc, w)))


def solution(mesh):
    return jax.shard_map(
        local,
        mesh=mesh,
        in_specs=(P(("row", "col"), None), P(), P(("row", "col")), P()),
        out_specs=(P("row", "col"), P("row", None)),
        check_vma=False,
    )
```

```python
import functools
import math

import jax
import jax.numpy as jnp
from jax import lax
from jax.experimental import pallas as pl
from jax.experimental.pallas import tpu as pltpu
from jax.sharding import PartitionSpec as P

MESH = pl.DeviceIdType.MESH
F = 128
B = 256
OWN = 192
BLOCK = 200
PIECE = 24
N_ROW = 8
N_COL = 16
NB = 32
TILE = 384
PT = 1536
PARTS = 1
MC = 512
STEPS = 8
COLS = 1536
HALF = 96
CHUNK = 512
W_AT = (2, 4)
SPANS = ((0, 512), (512, 1024), (1024, 1536), (1536, 1792))
FOLD = math.sqrt(5.0) / math.log(2.0)
LN2 = math.log(2.0)
BF16 = jnp.bfloat16
F32 = jnp.float32


def split2(a):
    high = a.astype(BF16)
    return high, (a - high.astype(F32)).astype(BF16)


def split3(a):
    high = a.astype(BF16)
    rest = a - high.astype(F32)
    mid = rest.astype(BF16)
    return high, mid, (rest - mid.astype(F32)).astype(BF16)


def mm(a, b):
    return jnp.dot(a, b, preferred_element_type=F32)


def left_parts(scaled):
    high, low = split2(scaled)
    return high, low, 0.25 * jnp.sum(scaled * scaled, axis=1, keepdims=True)


def left_ones(n):
    return jnp.where(lax.broadcasted_iota(jnp.int32, (n, F), 1) < 3, 1.0, 0.0).astype(BF16)


def right_operand(scaled_t):
    n = scaled_t.shape[1]
    sq = -jnp.sum(scaled_t * scaled_t, axis=0, keepdims=True)
    high, low = split2(scaled_t)
    one, two, three = (part.astype(F32) for part in split3(sq))
    sub = lax.broadcasted_iota(jnp.int32, (16, n), 0)
    extra = jnp.where(sub == 0, one, jnp.where(sub == 1, two, jnp.where(sub == 2, three, 0.0)))
    return jnp.concatenate(
        [high, high, low, extra.astype(BF16), jnp.zeros((F - 16, n), BF16)], axis=0
    )


def kernel_values(scaled2, right, signal):
    high, low, sq = left_parts(scaled2)
    left = jnp.concatenate([high, low, high, left_ones(scaled2.shape[0])], axis=1)
    return matern(sq - mm(left, right), signal)


def eye(n):
    return lax.broadcasted_iota(jnp.int32, (n, n), 0) == lax.broadcasted_iota(jnp.int32, (n, n), 1)


def rows_of(t):
    return pl.ds(pl.multiple_of(t * TILE, TILE), TILE)


def matern(u2, signal):
    start = jnp.log2(jnp.full((1, 1), LN2 * LN2 / 3.0, F32) * signal)
    a = jnp.maximum(u2, 1e-30)
    u = a * lax.rsqrt(a)
    v = u + 1.5 / LN2
    return (v * v + 0.75 / (LN2 * LN2)) * jnp.exp2(start - u)


def pivot_noise(tile0, tile1):
    first = tile0[0:1, :]
    second = jnp.concatenate([tile0[1:2, 0:64], tile1[0:1, 0:64]], axis=1)
    return jnp.concatenate([first, second], axis=1)


def remote(src, dst, send, recv, rr, cc):
    return pltpu.make_async_remote_copy(
        src_ref=src, dst_ref=dst, send_sem=send, recv_sem=recv,
        device_id=(rr, cc), device_id_type=MESH,
    )


def loop(low, high, body):
    def step(k, carry):
        body(k)
        return carry

    lax.fori_loop(low, high, step, 0)


def eliminate(aug, w_ref, between):
    sub8 = lax.broadcasted_iota(jnp.int32, (8, F), 0)

    def block_step(step, half):
        between(step)
        base = pl.multiple_of(step * NB, NB)
        shift = lax.rem(F - NB * lax.rem(step, 4), F)
        width = 3 * F
        span = slice(half * F, half * F + width)
        panel = [aug[pl.ds(base + 8 * g, 8), span] for g in range(4)]
        group = pltpu.roll(jnp.concatenate([part[:, 0:F] for part in panel], axis=0), shift, 1)
        rep = [
            [
                jnp.broadcast_to(group[8 * g:8 * g + 8, i:i + 1], (8, F)) if g >= i // 8 else None
                for g in range(4)
            ]
            for i in range(NB)
        ]
        root = []
        for j in range(NB):
            gj, sj = divmod(j, 8)
            pivot = jnp.broadcast_to(rep[j][gj][sj:sj + 1, :], (8, F))
            inverse = 1.0 / pivot
            root.append(lax.rsqrt(pivot))
            mult = [rep[j][g] * inverse if g >= gj else None for g in range(4)]
            for i in range(j + 1, NB):
                gi, si = divmod(i, 8)
                entry = jnp.broadcast_to(rep[j][gi][si:si + 1, :], (8, F))
                for g in range(gi, 4):
                    rep[i][g] = rep[i][g] - entry * mult[g]
            line = jnp.broadcast_to(panel[gj][sj:sj + 1, :], (8, width))
            for g in range(gj, 4):
                factor = mult[g]
                if g == gj:
                    factor = jnp.where(sub8 > sj, factor, 0.0)
                panel[g] = panel[g] - jnp.concatenate([factor] * 3, axis=1) * line
        out = []
        for g in range(4):
            scale_rows = root[8 * g]
            for s in range(1, 8):
                scale_rows = jnp.where(sub8 == s, root[8 * g + s], scale_rows)
            out.append(panel[g] * jnp.concatenate([scale_rows] * 3, axis=1))
        block = jnp.concatenate(out, axis=0)
        if half == 0:
            w_ref[pl.ds(base, NB), 0:F] = block[:, 2 * F:3 * F]
            w_ref[pl.ds(base, NB), F:B] = jnp.zeros((NB, F), F32)
            left = block[:, 0:B]
        else:
            w_ref[pl.ds(base, NB), :] = block[:, F:3 * F]
            left = block[:, 0:F]
        aug[half * F:B, span] -= jnp.dot(
            left.T, block, precision=lax.Precision.HIGHEST, preferred_element_type=F32
        )

    loop(0, 4, lambda step: block_step(step, 0))
    loop(4, 8, lambda step: block_step(step, 1))


def build_kernel(
    feat_hbm, noise_hbm, scale_hbm, signal_ref,
    k_ref, k_pc_ref, w_ref,
    rows_ref, cols_ref, piv_ref, stage, tail, zbuf, aug, noise_ref, scale_ref,
    right_d, left_d,
    in_sem, s1_send, s1_recv, s2_send, s2_recv, s3_send, s3_recv, tail_send, tail_recv,
    w1_send, w1_recv, w2_send, w2_recv, w3_send, w3_recv,
    p1_send, h0_send, h1_send, h0_recv, h1_recv,
    z_send, z_recv, xy_send, cols_recv, sib_send,
):
    r = lax.axis_index("row")
    c = lax.axis_index("col")
    z = r // 2
    core = r % 2
    x = c // 4
    y = c % 4
    sib = z * 2 + (1 - core)
    index = c % 8
    root = (r == 0) & (c == 0)

    in_copies = (
        pltpu.make_async_copy(feat_hbm, zbuf.at[z, pl.ds(0, OWN), :], in_sem.at[0]),
        pltpu.make_async_copy(feat_hbm, rows_ref.at[c], in_sem.at[1]),
        pltpu.make_async_copy(noise_hbm, noise_ref, in_sem.at[2]),
        pltpu.make_async_copy(scale_hbm, scale_ref, in_sem.at[3]),
    )
    for copy in in_copies:
        copy.start()

    barrier = pltpu.get_barrier_semaphore()

    def signal_to(rr, cc):
        pl.semaphore_signal(barrier, inc=1, device_id=(rr, cc), device_id_type=MESH)

    def greet_z(k):
        signal_to(((z + k) % 4) * 2, c)
        signal_to(((z + k) % 4) * 2 + 1, c)

    loop(1, N_COL, lambda k: signal_to(r, (c + k) % N_COL))
    loop(1, 4, greet_z)
    signal_to(sib, c)

    @pl.when((c // 2) % 2 != core)
    def _():
        loop(0, 4, lambda i: signal_to(sib, c % 2 * 8 + 2 * i + core))


    for copy in in_copies:
        copy.wait()
    zbuf[z, OWN:BLOCK, :] = jnp.zeros((BLOCK - OWN, F), F32)
    zbuf[z, OWN:OWN + 1, :] = noise_ref[0:1, 0:F]
    zbuf[z, OWN + 1:OWN + 2, 0:64] = noise_ref[0:1, F:OWN]

    @pl.when((r == 0) & (c < 2))
    def _():
        tile = zbuf[z, OWN:BLOCK, :]
        for q in range(12):
            stage[q, 0:16, :] = zbuf[z, 16 * q:16 * q + 16, :]
            stage[q, 16:PIECE, :] = tile

    @pl.when(index % 2 != core)
    def _():
        pl.semaphore_wait(barrier, 15 + 6 + 1 + 4)

    @pl.when(index % 2 == core)
    def _():
        pl.semaphore_wait(barrier, 15 + 6 + 1)

    tail_copy = remote(stage.at[pl.ds(0, 4)], tail, tail_send, tail_recv, 0, 0)

    def s1_copy(q, target):
        return remote(stage.at[q], piv_ref.at[target], s1_send.at[q], s1_recv, 0, target)

    @pl.when(root)
    def _():
        loop(1, 12, lambda q: s1_copy(q, q).start())
        piv_ref[0] = stage[0]

    @pl.when((r == 0) & (c == 1))
    def _():
        tail_copy.start()
        loop(0, 4, lambda q: s1_copy(q, 12 + q).start())

    def x_at(k):
        return ((x + k) % 4) * 4 + y

    def y_at(k):
        return x * 4 + (y + k) % 4

    def top(slot):
        return rows_ref.at[slot, pl.ds(0, HALF), :]

    def bottom(slot):
        return rows_ref.at[slot, pl.ds(HALF, HALF), :]

    def top_along_x(k):
        return remote(top(c), top(c), p1_send.at[k], h0_recv.at[c], r, x_at(k))

    def bottom_along_y(k):
        return remote(bottom(c), bottom(c), p1_send.at[4 + k], h1_recv.at[c], r, y_at(k))

    def top_along_y(i, k):
        slot = x_at(i)
        return remote(top(slot), top(slot), h0_send.at[4 * i + k], h0_recv.at[slot], r, y_at(k))

    def bottom_along_x(i, k):
        slot = y_at(i)
        return remote(bottom(slot), bottom(slot), h1_send.at[4 * i + k], h1_recv.at[slot], r, x_at(k))

    def wait_top(slot):
        remote(top(slot), top(slot), p1_send.at[0], h0_recv.at[slot], r, c).wait_recv()

    def wait_bottom(slot):
        remote(bottom(slot), bottom(slot), p1_send.at[0], h1_recv.at[slot], r, c).wait_recv()

    def z_copy(k, slot):
        return remote(
            zbuf.at[slot], zbuf.at[slot], z_send.at[k], z_recv.at[slot],
            ((z + k) % 4) * 2 + core, c,
        )

    to_row = 2 * z + index % 2

    def xy_each(k, act_near, act_far):
        source = (z + k) % 4
        target = 2 * (2 * source + core) + c // 8
        mine = (target == c) & (to_row == r)

        @pl.when(mine)
        def _():
            act_near(zbuf.at[source], cols_ref.at[index], cols_recv.at[index])

        @pl.when(jnp.logical_not(mine))
        def _():
            act_far(
                remote(
                    zbuf.at[source], cols_ref.at[index], xy_send.at[k], cols_recv.at[index],
                    to_row, target,
                )
            )

    def xy_go(k):
        xy_each(
            k,
            lambda src, dst, sem: pltpu.make_async_copy(src, dst, sem).start(),
            lambda copy: copy.start(),
        )

    def first_go(k):
        top_along_x(k).start()
        bottom_along_y(k).start()

    def second_go(i):
        def go(k):
            top_along_y(i, k).start()
            bottom_along_x(i, k).start()

        loop(1, 4, go)

    def rest_of_rows(order=(1, 3, 2)):
        for i in order:
            wait_top(x_at(i))
            wait_bottom(y_at(i))
            second_go(i)

    def rest_of_columns():
        for k in (1, 3, 2):
            z_copy(k, (z + k) % 4).wait_recv()
            xy_go(k)

    loop(1, 4, lambda k: z_copy(k, z).start())
    loop(1, 4, first_go)
    xy_go(0)
    second_go(0)

    def s2_copy(k):
        return remote(piv_ref.at[c], piv_ref.at[c], s2_send.at[k], s2_recv, k, c)

    @pl.when((r == 0) & (c != 0))
    def _():
        s1_copy(0, c).wait_recv()

    @pl.when((r == 0) & (c != 0))
    def _():
        loop(1, N_ROW, lambda k: s2_copy(k).start())

    def peer(k):
        return ((x + k // 4) % 4) * 4 + (y + k % 4) % 4

    def s3_copy(k, slot):
        return remote(
            piv_ref.at[slot], piv_ref.at[slot], s3_send.at[k], s3_recv.at[slot], r, peer(k)
        )

    @pl.when((r == 0) & (c != 0))
    def _():
        loop(1, N_COL, lambda k: s3_copy(k, c).start())

    def sib_copy(i):
        return remote(cols_ref.at[i], cols_ref.at[i], sib_send.at[i], cols_recv.at[i], sib, c)

    def wait_cols(i):
        pltpu.make_async_copy(zbuf.at[0], cols_ref.at[i], cols_recv.at[i]).wait()

    def hand_over(k):
        i = 2 * k + core
        wait_cols(i)
        sib_copy(i).start()

    def w_piece(p):
        return w_ref.at[pl.ds(pl.multiple_of(16 * p, 16), 16), :]

    def w1_copy(p):
        return remote(w_piece(p), w_piece(p), w1_send.at[p], w1_recv, 0, p)

    def w2_copy(k):
        return remote(w_piece(c), w_piece(c), w2_send.at[k], w2_recv, k, c)

    def w3_copy(k, p):
        return remote(w_piece(p), w_piece(p), w3_send.at[k], w3_recv.at[p], r, peer(k))

    def w3_each(k, act):
        @pl.when((r != 0) | (peer(k) != 0))
        def _():
            act(w3_copy(k, c))

    def w3_go(k):
        w3_each(k, lambda copy: copy.start())

    signal = signal_ref[0, 0]
    scale = lax.rsqrt(scale_ref[...]) * FOLD

    @pl.when(root)
    def _():
        tail_copy.wait_recv()
        pivots = jnp.concatenate(
            [zbuf[0, 0:OWN, :]] + [tail[q, 0:16, :] for q in range(4)], axis=0
        ) * scale
        diagonal = pivot_noise(stage[0, 16:PIECE, :], tail[0, 16:PIECE, :])
        block = kernel_values(2.0 * pivots, right_operand(pivots.T), signal)
        aug[:, 0:B] = block + jnp.where(eye(B), diagonal, 0.0)
        aug[:, B:2 * B] = jnp.where(eye(B), 1.0, 0.0)

        def between(step):
            @pl.when(step == 1)
            def _():
                loop(1, N_ROW, lambda k: s2_copy(k).start())
                loop(1, N_COL, lambda k: s3_copy(k, c).start())

            @pl.when(step == 2)
            def _():
                rest_of_columns()

            @pl.when(step == 5)
            def _():
                loop(0, 4, hand_over)
                rest_of_rows()

        eliminate(aug, w_ref, between)
        loop(1, N_COL, lambda p: w1_copy(p).start())

    @pl.when(jnp.logical_not(root))
    def _():
        rest_of_columns()

        @pl.when(r != 0)
        def _():
            s2_copy(0).wait_recv()
            loop(1, N_COL, lambda k: s3_copy(k, c).start())

        rest_of_rows((1,))
        loop(0, 4, hand_over)
        rest_of_rows((3, 2))

    loop(1, N_COL, lambda k: s3_copy(k, peer(k)).wait_recv())
    loop(0, 4, lambda k: wait_cols(2 * k + 1 - core))

    pivots = jnp.concatenate([piv_ref[p, 0:16, :] for p in range(16)], axis=0) * scale
    noise = pivot_noise(piv_ref[0, 16:PIECE, :], piv_ref[12, 16:PIECE, :])
    right_d[:, COLS:COLS + B] = right_operand(pivots.T)
    for i in range(4):
        pair = jnp.concatenate([cols_ref[2 * i, 0:OWN, :], cols_ref[2 * i + 1, 0:OWN, :]], axis=0)
        right_d[:, TILE * i:TILE * (i + 1)] = right_operand((pair * scale).T)
    k_pc_ref[...] = kernel_values(2.0 * pivots, right_d[:, 0:COLS], signal)

    @pl.when(c == 0)
    def _():
        k_pc_ref[:, 0:B] += jnp.where(eye(B), noise, 0.0)

    left_d[:, 3 * F:4 * F] = left_ones(TILE)

    def tile(k):
        turn = k // 2
        turn = turn + turn // 2 - 2 * (turn // 3)
        t = 2 * ((x + turn) % 4) + (y // 2 + k) % 2

        @pl.when((k == W_AT[0]) & (r == 0))
        def _():
            @pl.when(c != 0)
            def _():
                w1_copy(c).wait_recv()

            loop(1, N_ROW, lambda to: w2_copy(to).start())
            loop(1, N_COL, w3_go)

        @pl.when((k == W_AT[1]) & (r != 0))
        def _():
            w2_copy(0).wait_recv()
            loop(1, N_COL, w3_go)

        for m in range(2):
            slot = 2 * t + m

            @pl.when(slot % 4 != y)
            def _():
                wait_top(slot)

            @pl.when(slot // 4 != x)
            def _():
                wait_bottom(slot)

        pair = jnp.concatenate([rows_ref[2 * t], rows_ref[2 * t + 1]], axis=0)
        high, low, sq = left_parts(pair * (scale * 2.0))
        left_d[:, 0:F] = high
        left_d[:, F:2 * F] = low
        left_d[:, 2 * F:3 * F] = high
        for low_at, high_at in SPANS:
            u2 = sq - mm(left_d[...], right_d[:, low_at:high_at])
            k_ref[rows_of(t), low_at:high_at] = matern(u2, signal)

        first = t - (c % 2) * 4

        @pl.when((r == c // 2) & (first >= 0) & (first < 4))
        def _():
            at = pl.multiple_of(first * TILE, TILE)
            lines = []
            for m in range(2):
                noise_tile = cols_ref[2 * first + m, OWN:BLOCK, :]
                lines += [noise_tile[0:1, :], noise_tile[1:2, 0:64]]
            line = jnp.concatenate(lines, axis=1)
            k_ref[rows_of(t), pl.ds(at, TILE)] += jnp.where(eye(TILE), line, 0.0)

    loop(0, STEPS, tile)

    @pl.when(r == 0)
    def _():
        k_ref[0:B, COLS:COLS + B] += jnp.where(eye(B), noise, 0.0)

    @pl.when(jnp.logical_not(root))
    def _():
        loop(1, N_COL, lambda k: w3_copy(k, peer(k)).wait_recv())

    loop(1, N_COL, lambda k: w3_each(k, lambda copy: copy.wait_send()))

    def second_sent(i):
        def each(k):
            top_along_y(i, k).wait_send()
            bottom_along_x(i, k).wait_send()

        loop(1, 4, each)

    loop(0, 4, second_sent)

    def first_sent(k):
        top_along_x(k).wait_send()
        bottom_along_y(k).wait_send()
        z_copy(k, z).wait_send()

    loop(1, 4, first_sent)
    loop(1, N_COL, lambda k: s3_copy(k, c).wait_send())
    loop(0, 4, lambda k: xy_each(k, lambda src, dst, sem: None, lambda copy: copy.wait_send()))
    loop(0, 4, lambda k: sib_copy(2 * k + core).wait_send())

    @pl.when(root)
    def _():
        loop(1, 12, lambda q: s1_copy(q, q).wait_send())
        loop(1, N_COL, lambda p: w1_copy(p).wait_send())

    @pl.when((r == 0) & (c == 1))
    def _():
        tail_copy.wait_send()
        loop(0, 4, lambda q: s1_copy(q, 12 + q).wait_send())

    @pl.when(r == 0)
    def _():
        loop(1, N_ROW, lambda k: s2_copy(k).wait_send())
        loop(1, N_ROW, lambda k: w2_copy(k).wait_send())


def build(features, noise, scales, signal):
    vmem = pl.BlockSpec(memory_space=pltpu.VMEM)
    smem = pl.BlockSpec(memory_space=pltpu.SMEM)
    hbm = pl.BlockSpec(memory_space=pltpu.HBM)
    dma = pltpu.SemaphoreType.DMA
    return pl.pallas_call(
        build_kernel,
        out_shape=(
            pltpu.VMEM((N_COL * OWN, COLS + B), F32),
            pltpu.VMEM((B, COLS), F32),
            jax.ShapeDtypeStruct((B, B), F32),
        ),
        in_specs=[hbm, hbm, hbm, smem],
        out_specs=(vmem,) * 3,
        scratch_shapes=[
            pltpu.VMEM((N_COL, OWN, F), F32),
            pltpu.VMEM((8, BLOCK, F), F32),
            pltpu.VMEM((16, PIECE, F), F32),
            pltpu.VMEM((12, PIECE, F), F32),
            pltpu.VMEM((4, PIECE, F), F32),
            pltpu.VMEM((4, BLOCK, F), F32),
            pltpu.VMEM((B, 2 * B), F32),
            pltpu.VMEM((1, OWN), F32),
            pltpu.VMEM((1, F), F32),
            pltpu.VMEM((4 * F, COLS + B), BF16),
            pltpu.VMEM((TILE, 4 * F), BF16),
            dma((4,)), dma((12,)), dma, dma((8,)), dma, dma((16,)), dma((16,)), dma, dma,
            dma((16,)), dma, dma((8,)), dma, dma((16,)), dma((16,)),
            dma((8,)), dma((16,)), dma((16,)), dma((16,)), dma((16,)),
            dma((4,)), dma((4,)), dma((4,)), dma((8,)), dma((8,)),
        ],
        compiler_params=pltpu.CompilerParams(
            collective_id=0, has_side_effects=True, vmem_limit_bytes=28 * 1024 * 1024
        ),
        cost_estimate=pl.CostEstimate(flops=10**9, bytes_accessed=10**7, transcendentals=0),
    )(features, noise, scales, signal)


def apply_kernel(
    k_ref, k_pc_ref, w_ref,
    out_hbm, panel_hbm,
    right_p, right_w, left_p, panels, outs,
    out_sem, panel_sem,
):
    w = w_ref[...]
    wt_high, wt_low = split2(w.T)
    right_w[...] = jnp.concatenate([wt_high, wt_high, wt_low], axis=0)

    w_high, w_low = split2(w)
    left_w = jnp.concatenate([w_high, w_low, w_high], axis=1)
    for i in range(COLS // CHUNK):
        span = slice(CHUNK * i, CHUNK * (i + 1))
        k_high, k_low = split2(k_pc_ref[:, span])
        p_high, p_low = split2(mm(left_w, jnp.concatenate([k_high, k_high, k_low], axis=0)))
        right_p[0:B, span] = p_high
        right_p[B:2 * B, span] = p_high
        right_p[2 * B:3 * B, span] = p_low

    def prow(t):
        return pl.ds(pl.multiple_of(t * PT, PT), PT)

    def panel_copy(t):
        return pltpu.make_async_copy(
            panels.at[prow(t), :], panel_hbm.at[prow(t), :], panel_sem.at[t]
        )

    def panel_tile(t):
        k_high, k_low = split2(k_ref[prow(t), COLS:COLS + B])
        panel = mm(jnp.concatenate([k_high, k_low, k_high], axis=1), right_w[...])
        panels[prow(t), :] = panel
        p_high, p_low = split2(panel)
        left_p[prow(t), 0:B] = p_high
        left_p[prow(t), B:2 * B] = p_low
        left_p[prow(t), 2 * B:3 * B] = p_high
        panel_copy(t).start()

    loop(0, 3072 // PT, panel_tile)

    def out_copy(t, slot, i):
        part = TILE // PARTS
        rows = pl.ds(pl.multiple_of(t * TILE + part * i, 8), part)
        return pltpu.make_async_copy(
            outs.at[slot, pl.ds(part * i, part), :], out_hbm.at[rows, :], out_sem.at[slot, i]
        )

    def main(t):
        slot = t % 2

        @pl.when(t >= 2)
        def _():
            for i in range(PARTS):
                out_copy(t - 2, slot, i).wait()

        for i in range(COLS // MC):
            span = slice(MC * i, MC * (i + 1))
            outs[slot, :, span] = k_ref[rows_of(t), span] - mm(left_p[rows_of(t), :], right_p[:, span])
        for i in range(PARTS):
            out_copy(t, slot, i).start()

    loop(0, STEPS, main)
    loop(0, 3072 // PT, lambda t: panel_copy(t).wait())
    for t in (STEPS - 2, STEPS - 1):
        for i in range(PARTS):
            out_copy(t, t % 2, i).wait()


def apply_panel(k, k_pc, w):
    vmem = pl.BlockSpec(memory_space=pltpu.VMEM)
    hbm = pl.BlockSpec(memory_space=pltpu.HBM)
    dma = pltpu.SemaphoreType.DMA
    n = N_COL * OWN
    return pl.pallas_call(
        apply_kernel,
        out_shape=(jax.ShapeDtypeStruct((n, COLS), F32), jax.ShapeDtypeStruct((n, B), F32)),
        in_specs=[vmem, vmem, vmem],
        out_specs=(hbm, hbm),
        scratch_shapes=[
            pltpu.VMEM((3 * B, COLS), BF16),
            pltpu.VMEM((3 * B, B), BF16),
            pltpu.VMEM((n, 3 * B), BF16),
            pltpu.VMEM((n, B), F32),
            pltpu.VMEM((2, TILE, COLS), F32),
            dma((2, PARTS)), dma((STEPS,)),
        ],
        compiler_params=pltpu.CompilerParams(vmem_limit_bytes=28 * 1024 * 1024),
        cost_estimate=pl.CostEstimate(flops=8 * 10**9, bytes_accessed=25 * 10**6, transcendentals=0),
    )(k, k_pc, w)


def local(features, squared_scales, noise_var, signal):
    hbm = lambda a: pltpu.with_memory_space_constraint(a, pltpu.HBM)
    k, k_pc, w = build(
        hbm(features),
        hbm(noise_var.reshape(1, OWN)),
        hbm(squared_scales.reshape(1, F)),
        signal.reshape(1, 1),
    )
    return apply_panel(*(pltpu.with_memory_space_constraint(a, pltpu.VMEM) for a in (k, k_pc, w)))


def solution(mesh):
    return jax.shard_map(
        local,
        mesh=mesh,
        in_specs=(P(("row", "col"), None), P(), P(("row", "col")), P()),
        out_specs=(P("row", "col"), P("row", None)),
        check_vma=False,
    )
```
